1024 devices in a mesh: expert: 32 (over x, y_hi), mp: 8 (over z), dp: 4 (over y_lo, core).
Axes of the slice: x: 8, y: 8 (y_hi: 4, y_lo: 2; y = y_hi * 2 + y_lo), z: 8, core: 2. Of those that a mesh axis runs over, the one named last changes fastest.
Arguments:
- grad_out: bfloat16 [32768, 2048], P(('expert', 'dp')), may hold values from -1.5 to 1.5
- tokens: bfloat16 [32768, 2048], P(('expert', 'dp')), may hold values from -6 to 6
- gate: bfloat16 [32768], P(('expert', 'dp')), may hold values from 0.19921875 to 1
- expert_index: int32 [32768], P(('expert', 'dp')), may hold values from 0 to 31, as said below
- slot: int32 [32768], P(('expert', 'dp')), may hold values from 0 to 7, as said below
- kept: int32 [32768], P(('expert', 'dp')), may hold values from 0 to 1, as said below
- w_in: bfloat16 [32, 2048, 5120], P('expert', None, 'mp'), may hold values from -0.125 to 0.125
- w_out: bfloat16 [32, 5120, 2048], P('expert', 'mp'), may hold values from -0.078125 to 0.078125
Outputs:
- grad_tokens: bfloat16 [32768, 2048], P(('expert', 'dp'))
- grad_gate: bfloat16 [32768], P(('expert', 'dp'))
- grad_w_in: bfloat16 [32, 2048, 5120], P('expert', 'dp', 'mp')
- grad_w_out: bfloat16 [32, 5120, 2048], P('expert', 'mp', 'dp')
The draws below stay inside these ranges and needn't reach their ends.
Inputs may be any that keep to these rules, and one draw needn't show every extreme that they name: `expert_index`: in each group of 256 consecutive tokens, kept tokens of one expert have distinct slots, and some expert has exactly 8 kept tokens; which experts are busy is drawn from the seed. slot is 0 where kept is 0. A token of one group is kept exactly when fewer than 8 tokens of that group with the same expert come before it in a priority order drawn from the seed.
All inputs are finite; a program needn't handle non-finite values.
Results may differ from the reference program's by a relative error of at most 0.022.
Values may be sent and summed in bfloat16 or wider, within the bound.
No kernel may reach another device: no remote copies, remote signals or barrier semaphores. Data moves between devices by JAX's collectives and lax.ppermute only.
A program may use at most 64 MiB of HBM per device.

```python
import math
import jax
import jax.numpy as jnp
from jax import lax

D = 2048
FF = 5120
CAP = 8
TOK_DEV = 256
EXPERTS = 32
TOKENS = 32768
N_EXPERT = 32
N_MP = 8
N_DP = 4


def route_table(key):
    key_first, key_second, key_order, key_score = jax.random.split(key, 4)
    first = jax.random.randint(key_first, (TOKENS,), 0, EXPERTS)
    second = jax.random.randint(key_second, (TOKENS,), 0, EXPERTS)
    lowest = jnp.minimum(first, second)
    order = jax.random.permutation(key_order, EXPERTS).astype(jnp.int32)
    chosen = order[lowest].astype(jnp.int32)
    score = jax.random.randint(key_score, (TOKENS,), 0, 2 ** 20) * TOK_DEV + jnp.arange(TOKENS, dtype=jnp.int32) % TOK_DEV
    blocked = chosen.reshape(-1, TOK_DEV)
    scores = score.reshape(-1, TOK_DEV)
    same = blocked[:, :, None] == blocked[:, None, :]
    earlier = scores[:, None, :] < scores[:, :, None]
    rank = jnp.sum((same & earlier).astype(jnp.int32), axis=2).reshape(TOKENS)
    keep = (rank < CAP).astype(jnp.int32)
    place = jnp.where(rank < CAP, rank, 0).astype(jnp.int32)
    return (chosen, place, keep)


def draw_expert_index(key, part):
    table = route_table(key)
    return table[0]


def draw_slot(key, part):
    table = route_table(key)
    return table[1]


def draw_kept(key, part):
    table = route_table(key)
    return table[2]


def block_levels(rng, extent, pieces, least, largest):
    gain = 1.0
    for dim, shards_of in pieces:
        heights = jax.random.uniform(jax.random.fold_in(jax.random.fold_in(rng, 6), dim), (shards_of,), jnp.float32, least / len(pieces), largest / len(pieces))
        gain = gain * jnp.repeat(jnp.exp(heights), extent[dim] // shards_of).reshape((-1,) + (1,) * (len(extent) - 1 - dim))
    return gain


def scatter_about(rng, extent, scale, limit, pieces=(), kind=jnp.bfloat16):
    gain = block_levels(rng, extent, pieces, -0.22, 0.18) if pieces else 1.0
    values = jax.random.normal(rng, extent, jnp.float32) * scale * gain
    return jnp.minimum(jnp.maximum(values, -limit), limit).astype(kind)


def setup_inputs(seed: int = 0) -> dict:
    key_of = jax.random.split(jax.random.key(seed), 9)
    grad_out = scatter_about(key_of[0], (TOKENS, D), 0.25, 1.5, ((0, 128),))
    tokens = scatter_about(key_of[1], (TOKENS, D), 1.0, 6.0, ((0, 128),))
    gate = jnp.clip(0.19921875 + 0.80078125 * jax.random.uniform(key_of[2], (TOKENS,), jnp.float32) ** block_levels(key_of[2], (TOKENS,), ((0, 128),), -0.2, 0.2), 0.19921875, 1.0).astype(jnp.bfloat16)
    expert_index = draw_expert_index(jax.random.fold_in(key_of[8], 71), 0)
    slot = draw_slot(jax.random.fold_in(key_of[8], 71), 0)
    kept = draw_kept(jax.random.fold_in(key_of[8], 71), 0)
    w_in = scatter_about(key_of[6], (EXPERTS, D, FF), D ** -0.5, 0.125, ((0, 32), (2, 8)))
    w_out = scatter_about(key_of[7], (EXPERTS, FF, D), FF ** -0.5, 0.078125, ((0, 32), (1, 8)))
    return dict(grad_out=grad_out, tokens=tokens, gate=gate, expert_index=expert_index, slot=slot, kept=kept, w_in=w_in, w_out=w_out)


root_two_pi = math.sqrt(2.0 / math.pi)

def gelu_value(pre):
    inner = root_two_pi * (pre + 0.044715 * pre * pre * pre)
    return 0.5 * pre * (1.0 + jnp.tanh(inner))

def gelu_slope(pre):
    inner = root_two_pi * (pre + 0.044715 * pre * pre * pre)
    tangent = jnp.tanh(inner)
    return 0.5 * (1.0 + tangent) + 0.5 * pre * (1.0 - tangent * tangent) * root_two_pi * (1.0 + 3.0 * 0.044715 * pre * pre)

def rounded(value):
    return lax.optimization_barrier(value.astype(jnp.bfloat16)).astype(jnp.float32)

def expert_grads(inputs):
    x_rows, dy_rows, g_rows, weight_in, weight_out = inputs
    width = FF // N_MP
    rows = N_EXPERT * CAP
    sum_in = jnp.zeros((D, FF), jnp.float32)
    sum_out = jnp.zeros((FF, D), jnp.float32)
    token_list = []
    gate_list = []
    for group in range(N_DP):
        xr = x_rows[group]
        dyr = dy_rows[group]
        gr = g_rows[group].astype(jnp.float32)[:, None]
        pre = jnp.dot(xr, weight_in, preferred_element_type=jnp.float32)
        hidden = gelu_value(pre).astype(jnp.bfloat16)
        back = jnp.dot(dyr, weight_out.T, preferred_element_type=jnp.float32)
        grad_pre = (gr * back * gelu_slope(pre)).astype(jnp.bfloat16)
        scaled = (gr * dyr.astype(jnp.float32)).astype(jnp.bfloat16)
        sum_in = sum_in + rounded(jnp.dot(xr.T, grad_pre, preferred_element_type=jnp.float32))
        sum_out = sum_out + rounded(jnp.dot(hidden.T, scaled, preferred_element_type=jnp.float32))
        token_sum = jnp.zeros((rows, D), jnp.float32)
        gate_sum = jnp.zeros((rows,), jnp.float32)
        for piece in range(N_MP):
            low = piece * width
            high = low + width
            token_sum = token_sum + rounded(jnp.dot(grad_pre[:, low:high], weight_in[:, low:high].T, preferred_element_type=jnp.float32))
            gate_sum = gate_sum + rounded(lax.optimization_barrier(jnp.sum(hidden[:, low:high].astype(jnp.float32) * back[:, low:high], axis=1)))
        token_list.append(token_sum.astype(jnp.bfloat16))
        gate_list.append(gate_sum.astype(jnp.bfloat16))
    return (sum_in.astype(jnp.bfloat16), sum_out.astype(jnp.bfloat16), jnp.stack(token_list), jnp.stack(gate_list))

def reference(grad_out, tokens, gate, expert_index, slot, kept, w_in, w_out):
    groups = N_EXPERT * N_DP
    slots = EXPERTS * CAP
    position = (expert_index * CAP + slot).reshape(groups, TOK_DEV).astype(jnp.int32)
    live = (kept == 1).reshape(groups, TOK_DEV)
    target = jnp.where(live, position, slots).astype(jnp.int32)

    def fill(values, where_to):
        empty = jnp.zeros((slots + 1,) + values.shape[1:], values.dtype)
        return empty.at[where_to].set(values)[:slots]
    x_buf = jax.vmap(fill)(tokens.reshape(groups, TOK_DEV, D), target)
    dy_buf = jax.vmap(fill)(grad_out.reshape(groups, TOK_DEV, D), target)
    g_buf = jax.vmap(fill)(gate.reshape(groups, TOK_DEV), target)

    def by_expert(buffer):
        shaped = buffer.reshape((N_EXPERT, N_DP, EXPERTS, CAP) + buffer.shape[2:])
        order = (2, 1, 0, 3) + tuple(range(4, shaped.ndim))
        moved = jnp.transpose(shaped, order)
        return moved.reshape((EXPERTS, N_DP, N_EXPERT * CAP) + buffer.shape[2:])
    grad_w_in, grad_w_out, token_back, gate_back = lax.map(expert_grads, (by_expert(x_buf), by_expert(dy_buf), by_expert(g_buf), w_in, w_out))
    token_back = jnp.transpose(token_back.reshape(EXPERTS, N_DP, N_EXPERT, CAP, D), (2, 1, 0, 3, 4)).reshape(groups, slots, D)
    gate_back = jnp.transpose(gate_back.reshape(EXPERTS, N_DP, N_EXPERT, CAP), (2, 1, 0, 3)).reshape(groups, slots)

    def pick(buffer, where_from):
        return buffer[where_from]
    token_rows = jax.vmap(pick)(token_back, position)
    gate_rows = jax.vmap(pick)(gate_back, position)
    grad_tokens = jnp.where(live[:, :, None], token_rows, jnp.zeros((), jnp.bfloat16)).reshape(TOKENS, D)
    grad_gate = jnp.where(live, gate_rows, jnp.zeros((), jnp.bfloat16)).reshape(TOKENS)
    return (grad_tokens, grad_gate, grad_w_in, grad_w_out)
```

```python
import math

import jax
import jax.numpy as jnp
from jax import lax
from jax.sharding import PartitionSpec as P

D = 2048
CAP = 8
LANES = 128

root_two_pi = math.sqrt(2.0 / math.pi)


def gelu_pair(pre):
    inner = root_two_pi * (pre + 0.044715 * pre * pre * pre)
    tangent = jnp.tanh(inner)
    half = 0.5 * (1.0 + tangent)
    slope = half + 0.5 * pre * (1.0 - tangent * tangent) * root_two_pi * (
        1.0 + 3.0 * 0.044715 * pre * pre
    )
    return pre * half, slope


def dot(left, right, dims):
    return lax.dot_general(left, right, (dims, ((), ())), preferred_element_type=jnp.float32)


def shift(value, step):
    return lax.ppermute(value, "mp", [(i, (i + step) % 8) for i in range(8)])


def swap(value, bit):
    return lax.ppermute(value, "dp", [(i, i ^ bit) for i in range(4)])


def gather_pieces(piece):
    right, left, right2, left2 = (shift(piece, step) for step in (1, -1, 2, -2))
    half = piece.shape[0] // 2
    far = jnp.concatenate([shift(right2[:half], 2), shift(left2[half:], -2)])
    return [piece, right, left, right2, left2, shift(right2, 1), shift(left2, -1), far]


OFFSETS = (0, -1, 1, -2, 2, -3, 3, 4)


def local(grad_out, tokens, gate, expert_index, slot, kept, w_in, w_out):
    experts = lax.axis_size("expert")
    me = lax.axis_index("mp")
    data = lax.axis_index("dp")
    count = grad_out.shape[0]
    weight_in = w_in[0]
    weight_out = w_out[0]
    live = kept == 1
    gate_float = gate.astype(jnp.float32)

    position = expert_index * CAP + slot
    slots = experts * CAP
    pick = (
        (lax.broadcasted_iota(jnp.int32, (slots, count), 0) == position[None, :]) & live[None, :]
    ).astype(jnp.bfloat16)
    send = jnp.concatenate(
        [
            dot(pick, tokens, ((1,), (0,))).astype(jnp.bfloat16),
            dot(pick * gate[None, :], grad_out, ((1,), (0,))).astype(jnp.bfloat16),
        ],
        axis=1,
    )
    came = lax.all_to_all(
        send.reshape(experts, CAP, 2 * D), "expert", split_axis=0, concat_axis=0, tiled=True
    ).reshape(slots, 2 * D)
    x_rows = came[:, :D]
    s_rows = came[:, D:]

    pre = dot(x_rows, weight_in, ((1,), (0,)))
    value, slope = gelu_pair(pre)
    hidden = value.astype(jnp.bfloat16)
    back = dot(s_rows, weight_out, ((1,), (1,)))
    grad_pre = (back * slope).astype(jnp.bfloat16)
    gate_part = jnp.sum(hidden.astype(jnp.float32) * back, axis=1).astype(jnp.bfloat16)
    order = lax.broadcasted_iota(jnp.int32, (slots, slots), 0)
    order = order % experts * CAP + order // experts
    order = (order == lax.broadcasted_iota(jnp.int32, (slots, slots), 1)).astype(jnp.bfloat16)
    sorted_grad = dot(order, grad_pre, ((1,), (0,))).astype(jnp.bfloat16)
    sorted_gate = dot(
        order, jnp.broadcast_to(gate_part[:, None], (slots, LANES)), ((1,), (0,))
    ).astype(jnp.bfloat16)
    token_part = dot(sorted_grad, weight_in, ((1,), (1,))).astype(jnp.bfloat16)
    rows = jnp.concatenate([token_part, sorted_gate], axis=1)

    terms = lax.all_to_all(
        rows.reshape(CAP, experts, D + LANES), "mp", split_axis=0, concat_axis=0, tiled=True
    )
    total = jnp.sum(terms.astype(jnp.float32), axis=0)
    total = total.astype(jnp.bfloat16)
    home = lax.all_to_all(
        jnp.pad(total, ((0, 0), (0, LANES))).reshape(experts, 2, D // 2 + LANES),
        "expert", split_axis=0, concat_axis=0, tiled=True,
    ).reshape(experts, D + 2 * LANES)[:, : D + LANES]
    table = jnp.concatenate(gather_pieces(home))
    row_block = lax.broadcasted_iota(jnp.int32, (count, CAP * experts), 1) // experts
    row_expert = lax.broadcasted_iota(jnp.int32, (count, CAP * experts), 1) % experts
    ahead = (slot - me) & 7
    block = jnp.zeros_like(slot)
    for k, offset in enumerate(OFFSETS):
        block = jnp.where(ahead == offset % 8, k, block)
    choose = (
        (row_block == block[:, None]) & (row_expert == expert_index[:, None]) & live[:, None]
    ).astype(jnp.bfloat16)
    result = dot(choose, table, ((1,), (0,)))
    grad_tokens = result[:, :D].astype(jnp.bfloat16)
    grad_gate = (result[:, D] / gate_float).astype(jnp.bfloat16)

    def column(value, index):
        return lax.dynamic_slice_in_dim(value, index * (D // 4), D // 4, 1)

    def halves(value, mask):
        return column(value, data ^ mask), column(value, data ^ (mask ^ 2))

    x_keep, x_pass = halves(x_rows, 0)
    s_keep, s_pass = halves(s_rows, 0)
    other = swap(jnp.concatenate(halves(x_rows, 1) + halves(s_rows, 1), axis=1), 1)
    acts = jnp.concatenate([grad_pre, hidden], axis=1)
    other_acts = swap(acts, 1)
    width = grad_pre.shape[1]
    q = D // 4
    grads = jnp.concatenate([grad_pre, other_acts[:, :width]])
    hiddens = jnp.concatenate([hidden, other_acts[:, width:]])
    x_keep = jnp.concatenate([x_keep, other[:, :q]])
    x_pass = jnp.concatenate([x_pass, other[:, q : 2 * q]])
    s_keep = jnp.concatenate([s_keep, other[:, 2 * q : 3 * q]])
    s_pass = jnp.concatenate([s_pass, other[:, 3 * q :]])
    rows_first = ((0,), (0,))
    in_term = swap(dot(x_pass, grads, rows_first).astype(jnp.bfloat16), 2)
    out_term = swap(dot(hiddens, s_pass, rows_first).astype(jnp.bfloat16), 2)
    grad_w_in = (dot(x_keep, grads, rows_first) + in_term.astype(jnp.float32)).astype(jnp.bfloat16)[None]
    grad_w_out = (dot(hiddens, s_keep, rows_first) + out_term.astype(jnp.float32)).astype(jnp.bfloat16)[None]
    return (grad_tokens, grad_gate, grad_w_in, grad_w_out)


def solution(mesh):
    placed = (
        P(("expert", "dp"), None),
        P(("expert", "dp"), None),
        P(("expert", "dp")),
        P(("expert", "dp")),
        P(("expert", "dp")),
        P(("expert", "dp")),
        P("expert", None, "mp"),
        P("expert", "mp", None),
    )
    return jax.shard_map(
        local,
        mesh=mesh,
        in_specs=placed,
        out_specs=(
            P(("expert", "dp"), None),
            P(("expert", "dp")),
            P("expert", "dp", "mp"),
            P("expert", "mp", "dp"),
        ),
        check_vma=False,
    )
```

```python
import functools
import math

import jax
import jax.numpy as jnp
from jax import lax
from jax.experimental import pallas as pl
from jax.experimental.pallas import tpu as pltpu
from jax.sharding import PartitionSpec as P

CAP = 8
LANES = 128
MIB = 1 << 20
VMEM = pl.BlockSpec(memory_space=pltpu.VMEM)
ANY = pl.BlockSpec(memory_space=pl.ANY)
SMEM = pl.BlockSpec(memory_space=pltpu.SMEM)
BF16 = jnp.bfloat16
F32 = jnp.float32

root_two_pi = math.sqrt(2.0 / math.pi)


def gelu_pair(pre):
    inner = root_two_pi * (pre + 0.044715 * pre * pre * pre)
    tangent = jnp.tanh(inner)
    half = 0.5 * (1.0 + tangent)
    slope = half + 0.5 * pre * (1.0 - tangent * tangent) * root_two_pi * (
        1.0 + 3.0 * 0.044715 * pre * pre
    )
    return pre * half, slope


def dot(left, right, over_left, over_right):
    return lax.dot_general(
        left, right, (((over_left,), (over_right,)), ((), ())), preferred_element_type=F32
    )


def iota(shape, dim):
    return lax.broadcasted_iota(jnp.int32, shape, dim)


def params(mib):
    return pltpu.CompilerParams(vmem_limit_bytes=mib * MIB)


def cost(flops, moved):
    return pl.CostEstimate(flops=flops, bytes_accessed=moved, transcendentals=0)


def slot_hits(expert_ref, slot_ref, kept_ref, slots):
    position = jnp.where(kept_ref[...] == 1, expert_ref[...] * CAP + slot_ref[...], -1)
    return iota((slots, position.shape[1]), 0) == position


def dispatch_kernel(slots, expert_ref, slot_ref, kept_ref, gate_ref, tokens_ref, grad_ref, out_ref):
    step = pl.program_id(0)
    hits = slot_hits(expert_ref, slot_ref, kept_ref, slots)

    @pl.when(step < 4)
    def _():
        pick = jnp.where(hits, 1.0, 0.0).astype(BF16)
        out_ref[...] = dot(pick, tokens_ref[...], 1, 0).astype(BF16)

    @pl.when(step >= 4)
    def _():
        pick = jnp.where(hits, gate_ref[...], 0.0).astype(BF16)
        out_ref[...] = dot(pick, grad_ref[...], 1, 0).astype(BF16)


def dispatch(slots, index_rows, gate_row, tokens, grad_out):
    count, width = tokens.shape
    block = width // 4
    row = pl.BlockSpec((1, count), lambda i: (0, 0))
    return pl.pallas_call(
        functools.partial(dispatch_kernel, slots),
        grid=(8,),
        out_shape=jax.ShapeDtypeStruct((slots, 2 * width), BF16),
        in_specs=[row, row, row, row]
        + [
            pl.BlockSpec((count, block), lambda i: (0, jnp.minimum(i, 3))),
            pl.BlockSpec((count, block), lambda i: (0, jnp.maximum(i - 4, 0))),
        ],
        out_specs=pl.BlockSpec((slots, block), lambda i: (0, i)),
        compiler_params=params(56),
        cost_estimate=cost(4 * slots * count * width, 8 * slots * width),
    )(*index_rows, gate_row, tokens, grad_out)


def expert_kernel(data_ref, came, w_in, w_out, rows_ref, acts_ref, x_ref, s_ref, in_ref, out_ref, sems):
    slots, width = x_ref.shape
    hidden_width = in_ref.shape[1]
    quarter = width // 4
    copies = [
        pltpu.make_async_copy(came.at[:, :width], x_ref, sems.at[0]),
        pltpu.make_async_copy(w_in, in_ref, sems.at[1]),
        pltpu.make_async_copy(came.at[:, width:], s_ref, sems.at[2]),
        pltpu.make_async_copy(w_out, out_ref, sems.at[3]),
    ]
    for copy in copies:
        copy.start()
    copies[0].wait()
    copies[1].wait()
    pre = dot(x_ref[...], in_ref[...], 1, 0)
    value, slope = gelu_pair(pre)
    hidden = value.astype(BF16)
    acts_ref[:, width + hidden_width :] = hidden
    copies[2].wait()
    copies[3].wait()
    back = dot(s_ref[...], out_ref[...], 1, 1)
    grad_pre = (back * slope).astype(BF16)
    acts_ref[:, width : width + hidden_width] = grad_pre
    gate = jnp.sum(hidden.astype(F32) * back, axis=1, keepdims=True)
    same = iota((slots, slots), 0) == iota((slots, slots), 1)
    gate_row = jnp.sum(jnp.where(same, gate, 0.0), axis=0, keepdims=True)
    gate_rows = jnp.broadcast_to(gate_row, (16, slots)).astype(BF16)
    parts = rows_ref.shape[0]
    block = width // parts
    for part in range(parts):
        term = dot(grad_pre, in_ref[part * block : (part + 1) * block, :], 1, 1)
        rows_ref[part, :slots, :] = term.astype(BF16)
        rows_ref[part, slots:, :] = gate_rows
    for k, ref in enumerate((x_ref, x_ref, s_ref, s_ref)):
        index = data_ref[0] ^ (1, 3)[k % 2]
        place = pl.ds(pl.multiple_of(index * quarter, quarter), quarter)
        acts_ref[:, k * quarter : (k + 1) * quarter] = ref[:, place]


def expert(data, came, w_in, w_out, parts):
    slots = came.shape[0]
    width, hidden_width = w_in.shape
    return pl.pallas_call(
        expert_kernel,
        out_shape=(
            jax.ShapeDtypeStruct((parts, slots + 16, width // parts), BF16),
            jax.ShapeDtypeStruct((slots, width + 2 * hidden_width), BF16),
        ),
        in_specs=[SMEM, ANY, ANY, ANY],
        out_specs=(VMEM, VMEM),
        scratch_shapes=[
            pltpu.VMEM((slots, width), BF16),
            pltpu.VMEM((slots, width), BF16),
            pltpu.VMEM(w_in.shape, BF16),
            pltpu.VMEM(w_out.shape, BF16),
            pltpu.SemaphoreType.DMA((4,)),
        ],
        compiler_params=params(56),
        cost_estimate=cost(
            6 * slots * width * hidden_width, 4 * width * (slots + hidden_width) + 4 * slots * width
        ),
    )(data, came, w_in, w_out)


def sum_kernel(terms_ref, out_ref):
    slots = out_ref.shape[0]
    block = terms_ref.shape[2]
    total = terms_ref[0].astype(F32)
    for part in range(1, terms_ref.shape[0]):
        total = total + terms_ref[part].astype(F32)
    out_ref[:, :block] = total[:slots].astype(BF16)
    same = iota((slots, slots), 0) == iota((slots, slots), 1)
    gate = jnp.sum(jnp.where(same, total[slots : slots + 1], 0.0), axis=1, keepdims=True)
    out_ref[:, block:] = jnp.broadcast_to(gate, (slots, LANES)).astype(BF16)


def sum_terms(terms, slots):
    parts, _, block = terms.shape
    return pl.pallas_call(
        sum_kernel,
        out_shape=jax.ShapeDtypeStruct((slots, block + LANES), BF16),
        in_specs=[VMEM],
        out_specs=VMEM,
        compiler_params=params(56),
        cost_estimate=cost(parts * slots * block, 2 * parts * slots * block),
    )(terms)


def finish_kernel(me_ref, expert_ref, slot_ref, kept_ref, gate_ref, home_ref, *refs):
    same_ref, low_ref, high_ref, tokens_ref, gates_ref = refs
    slots, block = home_ref.shape[0], same_ref.shape[1]
    hits = slot_hits(expert_ref, slot_ref, kept_ref, slots)
    column = home_ref[:, block : block + 1].astype(F32)
    gates_ref[...] = jnp.sum(jnp.where(hits, column, 0.0), axis=0, keepdims=True) / gate_ref[...]
    choose = jnp.where(hits, 1.0, 0.0).T.astype(BF16)
    odd = me_ref[0] & 1

    def store(index, piece):
        place = pl.multiple_of(index * block, block)
        tokens_ref[:, pl.ds(place, block)] = dot(choose, piece, 1, 0).astype(BF16)

    for k in range(4):
        store(2 * k + odd, same_ref[k * slots : (k + 1) * slots, :])
    for k in range(2):
        store(2 * k + 1 - odd, low_ref[k * slots : (k + 1) * slots, :])
        store(2 * k + 5 - odd, high_ref[k * slots : (k + 1) * slots, :])


def finish(me, index_rows, gate_row, home, pieces, width):
    count = gate_row.shape[1]
    return pl.pallas_call(
        finish_kernel,
        out_shape=(
            jax.ShapeDtypeStruct((count, width), BF16),
            jax.ShapeDtypeStruct((1, count), F32),
        ),
        in_specs=[SMEM] + [VMEM] * (5 + len(pieces)),
        out_specs=(VMEM, VMEM),
        compiler_params=params(56),
        cost_estimate=cost(2 * count * count * width, 4 * count * width),
    )(me, *index_rows, gate_row, home, *pieces)


def weight_kernel(turn, place_ref, x_ref, s_ref, acts_ref, other_ref, *refs):
    added, (in_ref, out_ref) = refs[:-2], refs[-2:]
    quarter, width = in_ref.shape
    grads = slice(4 * quarter, 4 * quarter + width)
    hiddens = slice(4 * quarter + width, 4 * quarter + 2 * width)
    x_other = other_ref[:, turn * quarter : (turn + 1) * quarter]
    s_other = other_ref[:, (turn + 2) * quarter : (turn + 3) * quarter]
    first = dot(x_ref[...], acts_ref[:, grads], 0, 0) + dot(x_other, other_ref[:, grads], 0, 0)
    if added:
        first = first + added[0][...].astype(F32)
    in_ref[...] = first.astype(BF16)
    second = dot(acts_ref[:, hiddens], s_ref[...], 0, 0) + dot(other_ref[:, hiddens], s_other, 0, 0)
    if added:
        second = second + added[1][...].astype(F32)
    out_ref[...] = second.astype(BF16)


def weight_terms(turn, place, came, acts, other, added=()):
    slots = came.shape[0]
    quarter = came.shape[1] // 8
    width = (acts.shape[1] - 4 * quarter) // 2
    left = pl.BlockSpec((slots, quarter), lambda i, place: (0, place[0]))
    right = pl.BlockSpec((slots, quarter), lambda i, place: (0, place[0] + 4))
    whole = lambda shape: pl.BlockSpec(shape, lambda i, place: (0, 0))
    outs = ((quarter, width), (width, quarter))
    return pl.pallas_call(
        functools.partial(weight_kernel, turn),
        grid_spec=pltpu.PrefetchScalarGridSpec(
            num_scalar_prefetch=1,
            grid=(1,),
            in_specs=[left, right, whole(acts.shape), whole(acts.shape)]
            + [whole(a.shape) for a in added],
            out_specs=tuple(whole(shape) for shape in outs),
        ),
        out_shape=tuple(jax.ShapeDtypeStruct(shape, BF16) for shape in outs),
        compiler_params=params(56),
        cost_estimate=cost(8 * slots * quarter * width, 8 * slots * (quarter + width) + 4 * quarter * width),
    )(place, came, came, acts, other, *added)


def shift(value, step):
    return lax.ppermute(value, "mp", [(i, (i + step) % 8) for i in range(8)])


def swap(value, bit):
    return lax.ppermute(value, "dp", [(i, i ^ bit) for i in range(4)])


def gather_pieces(piece):
    same = lax.all_gather(
        piece, "mp", axis=0, tiled=True, axis_index_groups=[[0, 2, 4, 6], [1, 3, 5, 7]]
    )
    half = same.shape[0] // 2
    return same, shift(same[:half], 1), shift(same[half:], -1)


def scatter(value, axis):
    return lax.all_to_all(value, axis, split_axis=0, concat_axis=0, tiled=True)


def local(grad_out, tokens, gate, expert_index, slot, kept, w_in, w_out):
    experts = lax.axis_size("expert")
    parts = lax.axis_size("mp")
    count, width = tokens.shape
    slots = experts * CAP
    index_rows = [value.reshape(1, count) for value in (expert_index, slot, kept)]
    gate_row = gate.astype(F32).reshape(1, count)
    me = lax.axis_index("mp").astype(jnp.int32).reshape(1)
    data = lax.axis_index("dp").astype(jnp.int32).reshape(1)

    send = dispatch(slots, index_rows, gate_row, tokens, grad_out)
    came = scatter(send.reshape(experts, CAP, 2 * width), "expert").reshape(slots, 2 * width)
    rows, acts = expert(data, came, w_in[0], w_out[0], parts)
    terms = scatter(rows, "mp")

    other = swap(acts, 1)
    sends = weight_terms(1, data ^ 2, came, acts, other)
    added = [swap(value, 2) for value in sends]
    grad_w_in, grad_w_out = weight_terms(0, data, came, acts, other, added)

    total = sum_terms(terms, slots)
    home = scatter(total.reshape(experts, CAP, total.shape[1]), "expert").reshape(total.shape)
    home, (grad_w_in, grad_w_out) = lax.optimization_barrier((home, (grad_w_in, grad_w_out)))
    pieces = gather_pieces(home[:, : width // parts])
    grad_tokens, grad_gate = finish(me, index_rows, gate_row, home, pieces, width)
    return (grad_tokens, grad_gate.reshape(count).astype(BF16), grad_w_in[None], grad_w_out[None])


def solution(mesh):
    placed = (
        P(("expert", "dp"), None),
        P(("expert", "dp"), None),
        P(("expert", "dp")),
        P(("expert", "dp")),
        P(("expert", "dp")),
        P(("expert", "dp")),
        P("expert", None, "mp"),
        P("expert", "mp", None),
    )
    return jax.shard_map(
        local,
        mesh=mesh,
        in_specs=placed,
        out_specs=(
            P(("expert", "dp"), None),
            P(("expert", "dp")),
            P("expert", "dp", "mp"),
            P("expert", "mp", "dp"),
        ),
        check_vma=False,
    )
```

```python
import functools
import math

import jax
import jax.numpy as jnp
from jax import lax
from jax.experimental import pallas as pl
from jax.experimental.pallas import tpu as pltpu
from jax.sharding import PartitionSpec as P

CAP = 8
LANES = 128
MIB = 1 << 20
VMEM = pl.BlockSpec(memory_space=pltpu.VMEM)
ANY = pl.BlockSpec(memory_space=pl.ANY)
SMEM = pl.BlockSpec(memory_space=pltpu.SMEM)
BF16 = jnp.bfloat16
F32 = jnp.float32

root_two_pi = math.sqrt(2.0 / math.pi)


def gelu_pair(pre):
    inner = root_two_pi * (pre + 0.044715 * pre * pre * pre)
    tangent = jnp.tanh(inner)
    half = 0.5 * (1.0 + tangent)
    slope = half + 0.5 * pre * (1.0 - tangent * tangent) * root_two_pi * (
        1.0 + 3.0 * 0.044715 * pre * pre
    )
    return pre * half, slope


def dot(left, right, over_left, over_right):
    return lax.dot_general(
        left, right, (((over_left,), (over_right,)), ((), ())), preferred_element_type=F32
    )


def iota(shape, dim):
    return lax.broadcasted_iota(jnp.int32, shape, dim)


def params(mib):
    return pltpu.CompilerParams(vmem_limit_bytes=mib * MIB)


def cost(flops, moved):
    return pl.CostEstimate(flops=flops, bytes_accessed=moved, transcendentals=0)


def slot_hits(expert_ref, slot_ref, kept_ref, slots):
    position = jnp.where(kept_ref[...] == 1, expert_ref[...] * CAP + slot_ref[...], -1)
    return iota((slots, position.shape[1]), 0) == position


def dispatch_kernel(me_ref, expert_ref, slot_ref, kept_ref, gate_ref, tokens, grad_out, send_ref, x_ref, dy_ref, sems):
    rows, half = send_ref.shape
    loads = [
        pltpu.make_async_copy(tokens, x_ref, sems.at[0]),
        pltpu.make_async_copy(grad_out, dy_ref, sems.at[1]),
    ]
    for load in loads:
        load.start()
    position = jnp.where(kept_ref[...] == 1, expert_ref[...] * CAP + slot_ref[...], -1)
    shape = (rows, position.shape[1])
    row = iota(shape, 0)
    hits = (row & ~7) + (me_ref[0] & 3) + 4 * (row & 1) == position
    quarter = (row >> 1) & 3
    total = None
    for q, (ref, factor) in enumerate(
        ((x_ref, 1.0), (x_ref, 1.0), (dy_ref, gate_ref[...]), (dy_ref, gate_ref[...]))
    ):
        pick = jnp.where(hits & (quarter == q), factor, 0.0).astype(BF16)
        if q % 2 == 0:
            loads[q // 2].wait()
        low = (q % 2) * half
        term = dot(pick, ref[:, low : low + half], 1, 0)
        total = term if total is None else total + term
    send_ref[...] = total.astype(BF16)


def dispatch(me, slots, index_rows, gate_row, tokens, grad_out):
    count, width = tokens.shape
    return pl.pallas_call(
        dispatch_kernel,
        out_shape=jax.ShapeDtypeStruct((slots, width // 2), BF16),
        in_specs=[SMEM] + [VMEM] * 4 + [ANY] * 2,
        out_specs=VMEM,
        scratch_shapes=[
            pltpu.VMEM((count, width), BF16),
            pltpu.VMEM((count, width), BF16),
            pltpu.SemaphoreType.DMA((2,)),
        ],
        compiler_params=params(58),
        cost_estimate=cost(4 * slots * count * width, 5 * slots * width),
    )(me, *index_rows, gate_row, tokens, grad_out)


def expert_kernel(
    me_ref, data_ref, own, before, after, low, high, w_in, w_out, rows, acts, mine,
    packed, x_ref, s_ref, in_ref, out_ref, rows_ref, acts_ref, mine_ref, sems,
):
    slots, width = x_ref.shape
    hidden_width = in_ref.shape[1]
    quarter, half, part_rows = width // 4, slots // 2, slots // 4
    loads = [
        pltpu.make_async_copy(own, packed.at[0], sems.at[0]),
        pltpu.make_async_copy(before, packed.at[1], sems.at[1]),
        pltpu.make_async_copy(after, packed.at[2], sems.at[2]),
        pltpu.make_async_copy(low, packed.at[3, :half], sems.at[3]),
        pltpu.make_async_copy(high, packed.at[3, half:], sems.at[4]),
        pltpu.make_async_copy(w_in, in_ref, sems.at[5]),
        pltpu.make_async_copy(w_out, out_ref, sems.at[6]),
    ]
    for load in loads:
        load.start()
    square = (slots, slots)
    to, at = iota(square, 0), iota(square, 1)
    inner = to % part_rows
    unpack = jnp.where(at == (inner >> 1) * 8 + (to // part_rows) * 2 + (inner & 1), 1.0, 0.0).astype(BF16)
    for k, offset in enumerate((0, 3, 1, 2)):
        loads[k].wait()
        if k == 3:
            loads[4].wait()
        plain = dot(unpack, packed[k], 1, 0).astype(BF16)
        group = (me_ref[0] + offset) & 3
        place = pl.ds(pl.multiple_of(group * part_rows, part_rows), part_rows)
        for q, ref in enumerate((x_ref, x_ref, s_ref, s_ref)):
            first = (q % 2) * (width // 2)
            ref[place, first : first + width // 2] = plain[q * part_rows : (q + 1) * part_rows]
    loads[5].wait()
    pre = dot(x_ref[...], in_ref[...], 1, 0)
    value, slope = gelu_pair(pre)
    hidden = value.astype(BF16)
    acts_ref[:, width + hidden_width :] = hidden
    loads[6].wait()
    back = dot(s_ref[...], out_ref[...], 1, 1)
    grad_pre = (back * slope).astype(BF16)
    acts_ref[:, width : width + hidden_width] = grad_pre
    gate = jnp.sum(hidden.astype(F32) * back, axis=1, keepdims=True)
    gate_row = jnp.sum(jnp.where(to == at, gate, 0.0), axis=0, keepdims=True)
    gate_rows = jnp.broadcast_to(gate_row, (16, slots)).astype(BF16)
    parts = rows_ref.shape[0]
    block = width // parts
    stores = []
    for part in range(parts):
        term = dot(grad_pre, in_ref[part * block : (part + 1) * block, :], 1, 1)
        rows_ref[part, :slots, :] = term.astype(BF16)
        rows_ref[part, slots:, :] = gate_rows
        stores.append(pltpu.make_async_copy(rows_ref.at[part], rows.at[part], sems.at[7 + part]))
        stores[-1].start()
    for k, ref in enumerate((x_ref, x_ref, s_ref, s_ref)):
        for target, mask in ((mine_ref, (0, 2)[k % 2]), (acts_ref, (1, 3)[k % 2])):
            place = pl.ds(pl.multiple_of((data_ref[0] ^ mask) * quarter, quarter), quarter)
            target[:, k * quarter : (k + 1) * quarter] = ref[:, place]
    stores.append(pltpu.make_async_copy(acts_ref, acts, sems.at[7 + parts]))
    stores.append(pltpu.make_async_copy(mine_ref, mine, sems.at[8 + parts]))
    for store in stores[-2:]:
        store.start()
    for store in stores:
        store.wait()


def expert(me, data, packs, w_in, w_out, parts):
    slots = packs[0].shape[0]
    width, hidden_width = w_in.shape
    outs = (
        (parts, slots + 16, width // parts),
        (slots, width + 2 * hidden_width),
        (slots, width),
    )
    return pl.pallas_call(
        expert_kernel,
        out_shape=tuple(jax.ShapeDtypeStruct(shape, BF16) for shape in outs),
        in_specs=[SMEM, SMEM] + [ANY] * 7,
        out_specs=(ANY, ANY, ANY),
        scratch_shapes=[
            pltpu.VMEM((4, slots, width // 2), BF16),
            pltpu.VMEM((slots, width), BF16),
            pltpu.VMEM((slots, width), BF16),
            pltpu.VMEM(w_in.shape, BF16),
            pltpu.VMEM(w_out.shape, BF16),
        ]
        + [pltpu.VMEM(shape, BF16) for shape in outs]
        + [pltpu.SemaphoreType.DMA((9 + parts,))],
        compiler_params=params(59),
        cost_estimate=cost(
            6 * slots * width * hidden_width, 4 * width * (slots + hidden_width) + 8 * slots * width
        ),
    )(me, data, *packs, w_in, w_out)


def sum_kernel(terms_ref, out_ref):
    slots = out_ref.shape[0]
    block = terms_ref.shape[2]
    total = terms_ref[0].astype(F32)
    for part in range(1, terms_ref.shape[0]):
        total = total + terms_ref[part].astype(F32)
    to, at = iota((slots, slots), 0), iota((slots, slots), 1)
    from_row = (to & 3) * (slots // 4) + (to >> 3) * 2 + ((to >> 2) & 1)
    order = jnp.where(at == from_row, 1.0, 0.0)
    gate = jnp.sum(order * total[slots : slots + 1], axis=1, keepdims=True)
    sums = dot(order.astype(BF16), total[:slots].astype(BF16), 1, 0)
    out_ref[:, :block] = sums.astype(BF16)
    out_ref[:, block:] = jnp.broadcast_to(gate, (slots, LANES)).astype(BF16)


def sum_terms(terms, slots):
    parts, _, block = terms.shape
    return pl.pallas_call(
        sum_kernel,
        out_shape=jax.ShapeDtypeStruct((slots, block + LANES), BF16),
        in_specs=[VMEM],
        out_specs=VMEM,
        compiler_params=params(24),
        cost_estimate=cost(parts * slots * block, 2 * parts * slots * block),
    )(terms)


def finish_kernel(me_ref, expert_ref, slot_ref, kept_ref, gate_ref, home_ref, *refs):
    same_ref, low_ref, high_ref, tokens_ref, gates_ref = refs
    slots, block = home_ref.shape[0], same_ref.shape[1]
    hits = slot_hits(expert_ref, slot_ref, kept_ref, slots)
    column = home_ref[:, block : block + 1].astype(F32)
    gates_ref[...] = jnp.sum(jnp.where(hits, column, 0.0), axis=0, keepdims=True) / gate_ref[...]
    choose = jnp.where(hits, 1.0, 0.0).T.astype(BF16)
    odd = me_ref[0] & 1

    def store(index, piece):
        place = pl.multiple_of(index * block, block)
        tokens_ref[:, pl.ds(place, block)] = dot(choose, piece, 1, 0).astype(BF16)

    for k in range(4):
        store(2 * k + odd, same_ref[k * slots : (k + 1) * slots, :])
    for k in range(2):
        store(2 * k + 1 - odd, low_ref[k * slots : (k + 1) * slots, :])
        store(2 * k + 5 - odd, high_ref[k * slots : (k + 1) * slots, :])


def finish(me, index_rows, gate_row, home, pieces, width):
    count = gate_row.shape[1]
    return pl.pallas_call(
        finish_kernel,
        out_shape=(
            jax.ShapeDtypeStruct((count, width), BF16),
            jax.ShapeDtypeStruct((1, count), F32),
        ),
        in_specs=[SMEM] + [VMEM] * (5 + len(pieces)),
        out_specs=(VMEM, VMEM),
        compiler_params=params(24),
        cost_estimate=cost(2 * count * count * width, 4 * count * width),
    )(me, *index_rows, gate_row, home, *pieces)


def weight_kernel(turn, mine_ref, acts_ref, other_ref, *refs):
    added, (in_ref, out_ref) = refs[:-2], refs[-2:]
    quarter, width = in_ref.shape
    grads = slice(4 * quarter, 4 * quarter + width)
    hiddens = slice(4 * quarter + width, 4 * quarter + 2 * width)
    x_cols = slice(turn * quarter, (turn + 1) * quarter)
    s_cols = slice((turn + 2) * quarter, (turn + 3) * quarter)
    first = dot(mine_ref[:, x_cols], acts_ref[:, grads], 0, 0)
    first = first + dot(other_ref[:, x_cols], other_ref[:, grads], 0, 0)
    if added:
        first = first + added[0][...].astype(F32)
    in_ref[...] = first.astype(BF16)
    second = dot(acts_ref[:, hiddens], mine_ref[:, s_cols], 0, 0)
    second = second + dot(other_ref[:, hiddens], other_ref[:, s_cols], 0, 0)
    if added:
        second = second + added[1][...].astype(F32)
    out_ref[...] = second.astype(BF16)


def weight_terms(turn, mine, acts, other, added=()):
    slots = mine.shape[0]
    quarter = mine.shape[1] // 4
    width = (acts.shape[1] - 4 * quarter) // 2
    return pl.pallas_call(
        functools.partial(weight_kernel, turn),
        in_specs=[VMEM] * (3 + len(added)),
        out_specs=(VMEM, VMEM),
        out_shape=(
            jax.ShapeDtypeStruct((quarter, width), BF16),
            jax.ShapeDtypeStruct((width, quarter), BF16),
        ),
        compiler_params=params(24),
        cost_estimate=cost(8 * slots * quarter * width, 8 * slots * (quarter + width) + 4 * quarter * width),
    )(mine, acts, other, *added)


def shift(value, step):
    return lax.ppermute(value, "mp", [(i, (i + step) % 8) for i in range(8)])


def swap(value, bit):
    return lax.ppermute(value, "dp", [(i, i ^ bit) for i in range(4)])


def gather_pieces(piece):
    same = lax.all_gather(
        piece, "mp", axis=0, tiled=True, axis_index_groups=[[0, 2, 4, 6], [1, 3, 5, 7]]
    )
    half = same.shape[0] // 2
    return same, shift(same[:half], 1), shift(same[half:], -1)


def scatter(value, axis):
    return lax.all_to_all(value, axis, split_axis=0, concat_axis=0, tiled=True)


def local(grad_out, tokens, gate, expert_index, slot, kept, w_in, w_out):
    experts = lax.axis_size("expert")
    parts = lax.axis_size("mp")
    count, width = tokens.shape
    slots = experts * CAP
    index_rows = [value.reshape(1, count) for value in (expert_index, slot, kept)]
    gate_row = gate.astype(F32).reshape(1, count)
    me = lax.axis_index("mp").astype(jnp.int32).reshape(1)
    data = lax.axis_index("dp").astype(jnp.int32).reshape(1)

    send = dispatch(me, slots, index_rows, gate_row, tokens, grad_out)
    came = scatter(send.reshape(experts, CAP, width // 2), "expert").reshape(send.shape)
    packs = (came, shift(came, 1), shift(came, -1), shift(came[: slots // 2], 2), shift(came[slots // 2 :], -2))
    rows, acts, mine = expert(me, data, packs, w_in[0], w_out[0], parts)
    terms = scatter(rows, "mp")

    other = swap(acts, 1)
    added = [swap(value, 2) for value in weight_terms(1, mine, acts, other)]

    total = sum_terms(terms, slots)
    home = scatter(total.reshape(experts, CAP, total.shape[1]), "expert").reshape(total.shape)
    home, added = lax.optimization_barrier((home, added))
    grad_w_in, grad_w_out = weight_terms(0, mine, acts, other, added)
    pieces = gather_pieces(home[:, : width // parts])
    grad_tokens, grad_gate = finish(me, index_rows, gate_row, home, pieces, width)
    return (grad_tokens, grad_gate.reshape(count).astype(BF16), grad_w_in[None], grad_w_out[None])


def solution(mesh):
    placed = (
        P(("expert", "dp"), None),
        P(("expert", "dp"), None),
        P(("expert", "dp")),
        P(("expert", "dp")),
        P(("expert", "dp")),
        P(("expert", "dp")),
        P("expert", None, "mp"),
        P("expert", "mp", None),
    )
    return jax.shard_map(
        local,
        mesh=mesh,
        in_specs=placed,
        out_specs=(
            P(("expert", "dp"), None),
            P(("expert", "dp")),
            P("expert", "dp", "mp"),
            P("expert", "mp", "dp"),
        ),
        check_vma=False,
    )
```

```python
import functools
import math

import jax
import jax.numpy as jnp
from jax import lax
from jax.experimental import pallas as pl
from jax.experimental.pallas import tpu as pltpu
from jax.sharding import PartitionSpec as P

CAP = 8
LANES = 128
MIB = 1 << 20
VMEM = pl.BlockSpec(memory_space=pltpu.VMEM)
ANY = pl.BlockSpec(memory_space=pl.ANY)
SMEM = pl.BlockSpec(memory_space=pltpu.SMEM)
BF16 = jnp.bfloat16
PARITIES = [[0, 2, 4, 6], [1, 3, 5, 7]]
F32 = jnp.float32

root_two_pi = math.sqrt(2.0 / math.pi)


def gelu_pair(pre):
    inner = root_two_pi * (pre + 0.044715 * pre * pre * pre)
    tangent = jnp.tanh(inner)
    half = 0.5 * (1.0 + tangent)
    slope = half + 0.5 * pre * (1.0 - tangent * tangent) * root_two_pi * (
        1.0 + 3.0 * 0.044715 * pre * pre
    )
    return pre * half, slope


def dot(left, right, over_left, over_right):
    return lax.dot_general(
        left, right, (((over_left,), (over_right,)), ((), ())), preferred_element_type=F32
    )


def iota(shape, dim):
    return lax.broadcasted_iota(jnp.int32, shape, dim)


def params(mib):
    return pltpu.CompilerParams(vmem_limit_bytes=mib * MIB)


def cost(flops, moved):
    return pl.CostEstimate(flops=flops, bytes_accessed=moved, transcendentals=0)


def slot_hits(expert_ref, slot_ref, kept_ref, slots):
    position = jnp.where(kept_ref[...] == 1, expert_ref[...] * CAP + slot_ref[...], -1)
    return iota((slots, position.shape[1]), 0) == position


def dispatch_kernel(me_ref, expert_ref, slot_ref, kept_ref, gate_ref, tokens, grad_out, send_ref, x_ref, dy_ref, sems):
    rows, half = send_ref.shape
    loads = [
        pltpu.make_async_copy(tokens, x_ref, sems.at[0]),
        pltpu.make_async_copy(grad_out, dy_ref, sems.at[1]),
    ]
    for load in loads:
        load.start()
    position = jnp.where(kept_ref[...] == 1, expert_ref[...] * CAP + slot_ref[...], -1)
    shape = (rows, position.shape[1])
    row = iota(shape, 0)
    hits = (row & ~7) + (me_ref[0] & 3) + 4 * (row & 1) == position
    quarter = (row >> 1) & 3
    gate_row = gate_ref[...].astype(F32).reshape(1, -1)
    total = None
    for q, (ref, factor) in enumerate(
        ((x_ref, 1.0), (x_ref, 1.0), (dy_ref, gate_row), (dy_ref, gate_row))
    ):
        pick = jnp.where(hits & (quarter == q), factor, 0.0).astype(BF16)
        if q % 2 == 0:
            loads[q // 2].wait()
        low = (q % 2) * half
        term = dot(pick, ref[:, low : low + half], 1, 0)
        total = term if total is None else total + term
    send_ref[...] = total.astype(BF16)


def dispatch(me, slots, index_rows, gate, tokens, grad_out):
    count, width = tokens.shape
    return pl.pallas_call(
        dispatch_kernel,
        out_shape=jax.ShapeDtypeStruct((slots, width // 2), BF16),
        in_specs=[SMEM] + [VMEM] * 4 + [ANY] * 2,
        out_specs=VMEM,
        scratch_shapes=[
            pltpu.VMEM((count, width), BF16),
            pltpu.VMEM((count, width), BF16),
            pltpu.SemaphoreType.DMA((2,)),
        ],
        compiler_params=params(58),
        cost_estimate=cost(4 * slots * count * width, 5 * slots * width),
    )(me, *index_rows, gate, tokens, grad_out)


def expert_kernel(
    me_ref, data_ref, own, before, after, low, high, w_in, w_out, same, first, second, acts, mine,
    packed, x_ref, s_ref, in_ref, out_ref, rows_ref, acts_ref, mine_ref, sems,
):
    slots, width = x_ref.shape
    hidden_width = in_ref.shape[1]
    quarter, half, part_rows = width // 4, slots // 2, slots // 4
    parts = rows_ref.shape[0]
    loads = [
        pltpu.make_async_copy(own, packed.at[0], sems.at[0]),
        pltpu.make_async_copy(before, packed.at[1], sems.at[1]),
        pltpu.make_async_copy(after, packed.at[2], sems.at[2]),
        pltpu.make_async_copy(low, packed.at[3, :half], sems.at[3]),
        pltpu.make_async_copy(high, packed.at[3, half:], sems.at[4]),
        pltpu.make_async_copy(w_in, in_ref, sems.at[5]),
        pltpu.make_async_copy(w_out, out_ref, sems.at[6]),
    ]
    for load in loads:
        load.start()
    square = (slots, slots)
    to, at = iota(square, 0), iota(square, 1)
    inner = to % part_rows
    unpack = jnp.where(at == (inner >> 1) * 8 + (to // part_rows) * 2 + (inner & 1), 1.0, 0.0).astype(BF16)
    for k, offset in enumerate((0, 3, 1, 2)):
        loads[k].wait()
        if k == 3:
            loads[4].wait()
        plain = dot(unpack, packed[k], 1, 0).astype(BF16)
        group = (me_ref[0] + offset) & 3
        place = pl.ds(pl.multiple_of(group * part_rows, part_rows), part_rows)
        for q, ref in enumerate((x_ref, x_ref, s_ref, s_ref)):
            start = (q % 2) * (width // 2)
            ref[place, start : start + width // 2] = plain[q * part_rows : (q + 1) * part_rows]
    for k, ref in enumerate((x_ref, x_ref, s_ref, s_ref)):
        for target, mask in ((mine_ref, (0, 2)[k % 2]), (acts_ref, (1, 3)[k % 2])):
            place = pl.ds(pl.multiple_of((data_ref[0] ^ mask) * quarter, quarter), quarter)
            target[:, k * quarter : (k + 1) * quarter] = ref[:, place]
    stores = [
        pltpu.make_async_copy(mine_ref, mine, sems.at[7 + parts]),
        pltpu.make_async_copy(acts_ref, acts, sems.at[8 + parts]),
    ]
    stores[0].start()
    loads[5].wait()
    pre = dot(x_ref[...], in_ref[...], 1, 0)
    value, slope = gelu_pair(pre)
    hidden = value.astype(BF16)
    acts_ref[:, width + hidden_width :] = hidden
    loads[6].wait()
    back = dot(s_ref[...], out_ref[...], 1, 1)
    grad_pre = (back * slope).astype(BF16)
    acts_ref[:, width : width + hidden_width] = grad_pre
    stores[1].start()
    gate = jnp.sum(hidden.astype(F32) * back, axis=1, keepdims=True)
    gate_row = jnp.sum(jnp.where(to == at, gate, 0.0), axis=0, keepdims=True)
    gate_rows = jnp.broadcast_to(gate_row, (16, slots)).astype(BF16)
    block = width // parts
    odd = me_ref[0] & 1
    half_parts = parts // 2
    for part in range(parts):
        index = 2 * (part % half_parts) + (odd if part >= half_parts else 1 - odd)
        place = pl.ds(pl.multiple_of(index * block, block), block)
        rows_ref[part, :slots, :] = dot(grad_pre, in_ref[place, :], 1, 1).astype(BF16)
        rows_ref[part, slots:, :] = gate_rows
        if part >= half_parts:
            target = same.at[part - half_parts]
        else:
            target = (first, second)[part // 2].at[part % 2]
        stores.append(pltpu.make_async_copy(rows_ref.at[part], target, sems.at[7 + part]))
        stores[-1].start()
    for store in stores:
        store.wait()


def expert(me, data, packs, w_in, w_out, parts):
    slots = packs[0].shape[0]
    width, hidden_width = w_in.shape
    rows = (slots + 16, width // parts)
    outs = (
        (parts // 2,) + rows,
        (2,) + rows,
        (2,) + rows,
        (slots, width + 2 * hidden_width),
        (slots, width),
    )
    return pl.pallas_call(
        expert_kernel,
        out_shape=tuple(jax.ShapeDtypeStruct(shape, BF16) for shape in outs),
        in_specs=[SMEM, SMEM] + [ANY] * 7,
        out_specs=(ANY,) * 5,
        scratch_shapes=[
            pltpu.VMEM((4, slots, width // 2), BF16),
            pltpu.VMEM((slots, width), BF16),
            pltpu.VMEM((slots, width), BF16),
            pltpu.VMEM(w_in.shape, BF16),
            pltpu.VMEM(w_out.shape, BF16),
        ]
        + [pltpu.VMEM(shape, BF16) for shape in ((parts,) + rows,) + outs[3:]]
        + [pltpu.SemaphoreType.DMA((9 + parts,))],
        compiler_params=params(59),
        cost_estimate=cost(
            6 * slots * width * hidden_width, 4 * width * (slots + hidden_width) + 8 * slots * width
        ),
    )(me, data, *packs, w_in, w_out)


def add_kernel(same_ref, first_ref, second_ref, out_ref):
    for k in range(4):
        other = (first_ref, second_ref)[k // 2]
        out_ref[k] = (same_ref[k].astype(F32) + other[k % 2].astype(F32)).astype(BF16)


def add_terms(same, first, second):
    return pl.pallas_call(
        add_kernel,
        out_shape=jax.ShapeDtypeStruct(same.shape, BF16),
        in_specs=[VMEM] * 3,
        out_specs=VMEM,
        compiler_params=params(24),
        cost_estimate=cost(same.size, 6 * same.size),
    )(same, first, second)


def sum_kernel(terms_ref, out_ref):
    slots = out_ref.shape[0]
    block = terms_ref.shape[2]
    total = terms_ref[0].astype(F32)
    for part in range(1, terms_ref.shape[0]):
        total = total + terms_ref[part].astype(F32)
    to, at = iota((slots, slots), 0), iota((slots, slots), 1)
    from_row = (to & 3) * (slots // 4) + (to >> 3) * 2 + ((to >> 2) & 1)
    order = jnp.where(at == from_row, 1.0, 0.0)
    gate = jnp.sum(order * total[slots : slots + 1], axis=1, keepdims=True)
    sums = dot(order.astype(BF16), total[:slots].astype(BF16), 1, 0)
    out_ref[:, :block] = sums.astype(BF16)
    out_ref[:, block:] = jnp.broadcast_to(gate, (slots, LANES)).astype(BF16)


def sum_terms(terms, slots):
    parts, _, block = terms.shape
    return pl.pallas_call(
        sum_kernel,
        out_shape=jax.ShapeDtypeStruct((slots, block + LANES), BF16),
        in_specs=[VMEM],
        out_specs=VMEM,
        compiler_params=params(24),
        cost_estimate=cost(parts * slots * block, 2 * parts * slots * block),
    )(terms)


def finish_kernel(me_ref, expert_ref, slot_ref, kept_ref, gate_ref, home_ref, *refs):
    same_ref, low_ref, high_ref, tokens_ref, gates_ref = refs
    slots, block = home_ref.shape[0], same_ref.shape[1]
    hits = slot_hits(expert_ref, slot_ref, kept_ref, slots)
    column = home_ref[:, block : block + 1].astype(F32)
    picked = jnp.sum(jnp.where(hits, column, 0.0), axis=0, keepdims=True)
    gate_row = gate_ref[...].astype(F32).reshape(1, -1)
    gates_ref[...] = (picked / gate_row).astype(BF16).reshape(-1)
    choose = jnp.where(hits, 1.0, 0.0).T.astype(BF16)
    odd = me_ref[0] & 1

    def store(index, piece):
        place = pl.multiple_of(index * block, block)
        tokens_ref[:, pl.ds(place, block)] = dot(choose, piece, 1, 0).astype(BF16)

    for k in range(4):
        store(2 * k + odd, same_ref[k * slots : (k + 1) * slots, :])
    for k in range(2):
        store(2 * k + 1 - odd, low_ref[k * slots : (k + 1) * slots, :])
        store(2 * k + 5 - odd, high_ref[k * slots : (k + 1) * slots, :])


def finish(me, index_rows, gate, home, pieces, width):
    count = gate.shape[0]
    return pl.pallas_call(
        finish_kernel,
        out_shape=(
            jax.ShapeDtypeStruct((count, width), BF16),
            jax.ShapeDtypeStruct((count,), BF16),
        ),
        in_specs=[SMEM] + [VMEM] * (5 + len(pieces)),
        out_specs=(VMEM, VMEM),
        compiler_params=params(24),
        cost_estimate=cost(2 * count * count * width, 4 * count * width),
    )(me, *index_rows, gate, home, *pieces)


def weight_kernel(turn, mine_ref, acts_ref, other_ref, *refs):
    added, (in_ref, out_ref) = refs[:-2], refs[-2:]
    quarter, width = in_ref.shape
    grads = slice(4 * quarter, 4 * quarter + width)
    hiddens = slice(4 * quarter + width, 4 * quarter + 2 * width)
    x_cols = slice(turn * quarter, (turn + 1) * quarter)
    s_cols = slice((turn + 2) * quarter, (turn + 3) * quarter)
    first = dot(mine_ref[:, x_cols], acts_ref[:, grads], 0, 0)
    first = first + dot(other_ref[:, x_cols], other_ref[:, grads], 0, 0)
    if added:
        first = first + added[0][...].astype(F32)
    in_ref[...] = first.astype(BF16)
    second = dot(acts_ref[:, hiddens], mine_ref[:, s_cols], 0, 0)
    second = second + dot(other_ref[:, hiddens], other_ref[:, s_cols], 0, 0)
    if added:
        second = second + added[1][...].astype(F32)
    out_ref[...] = second.astype(BF16)


def weight_terms(turn, mine, acts, other, added=()):
    slots = mine.shape[0]
    quarter = mine.shape[1] // 4
    width = (acts.shape[1] - 4 * quarter) // 2
    return pl.pallas_call(
        functools.partial(weight_kernel, turn),
        in_specs=[VMEM] * (3 + len(added)),
        out_specs=(VMEM, VMEM),
        out_shape=(
            jax.ShapeDtypeStruct((quarter, width), BF16),
            jax.ShapeDtypeStruct((width, quarter), BF16),
        ),
        compiler_params=params(24),
        cost_estimate=cost(8 * slots * quarter * width, 8 * slots * (quarter + width) + 4 * quarter * width),
    )(mine, acts, other, *added)


def shift(value, step):
    return lax.ppermute(value, "mp", [(i, (i + step) % 8) for i in range(8)])


def swap(value, bit):
    return lax.ppermute(value, "dp", [(i, i ^ bit) for i in range(4)])


def gather_pieces(piece):
    same = lax.all_gather(
        piece, "mp", axis=0, tiled=True, axis_index_groups=PARITIES
    )
    half = same.shape[0] // 2
    return same, shift(same[:half], 1), shift(same[half:], -1)


def scatter(value, axis):
    return lax.all_to_all(value, axis, split_axis=0, concat_axis=0, tiled=True)


def local(grad_out, tokens, gate, expert_index, slot, kept, w_in, w_out):
    experts = lax.axis_size("expert")
    parts = lax.axis_size("mp")
    count, width = tokens.shape
    slots = experts * CAP
    index_rows = [value.reshape(1, count) for value in (expert_index, slot, kept)]
    me = lax.axis_index("mp").astype(jnp.int32).reshape(1)
    data = lax.axis_index("dp").astype(jnp.int32).reshape(1)

    send = dispatch(me, slots, index_rows, gate, tokens, grad_out)
    came = scatter(send.reshape(experts, CAP, width // 2), "expert").reshape(send.shape)
    packs = (came, shift(came, 1), shift(came, -1), shift(came[: slots // 2], 2), shift(came[slots // 2 :], -2))
    same, first, second, acts, mine = expert(me, data, packs, w_in[0], w_out[0], parts)
    pairs = add_terms(same, shift(first, 1), shift(second, -1))
    terms = lax.all_to_all(pairs, "mp", 0, 0, axis_index_groups=PARITIES, tiled=True)

    other = swap(acts, 1)
    added = [swap(value, 2) for value in weight_terms(1, mine, acts, other)]

    total = sum_terms(terms, slots)
    home = scatter(total.reshape(experts, CAP, total.shape[1]), "expert").reshape(total.shape)
    home, added = lax.optimization_barrier((home, added))
    grad_w_in, grad_w_out = weight_terms(0, mine, acts, other, added)
    pieces = gather_pieces(home[:, : width // parts])
    grad_tokens, grad_gate = finish(me, index_rows, gate, home, pieces, width)
    return (grad_tokens, grad_gate, grad_w_in[None], grad_w_out[None])


def solution(mesh):
    placed = (
        P(("expert", "dp"), None),
        P(("expert", "dp"), None),
        P(("expert", "dp")),
        P(("expert", "dp")),
        P(("expert", "dp")),
        P(("expert", "dp")),
        P("expert", None, "mp"),
        P("expert", "mp", None),
    )
    return jax.shard_map(
        local,
        mesh=mesh,
        in_specs=placed,
        out_specs=(
            P(("expert", "dp"), None),
            P(("expert", "dp")),
            P("expert", "dp", "mp"),
            P("expert", "mp", "dp"),
        ),
        check_vma=False,
    )
```

```python
import functools
import math

import jax
import jax.numpy as jnp
from jax import lax
from jax.experimental import pallas as pl
from jax.experimental.pallas import tpu as pltpu
from jax.sharding import PartitionSpec as P

CAP = 8
LANES = 128
MIB = 1 << 20
VMEM = pl.BlockSpec(memory_space=pltpu.VMEM)
ANY = pl.BlockSpec(memory_space=pl.ANY)
SMEM = pl.BlockSpec(memory_space=pltpu.SMEM)
BF16 = jnp.bfloat16
F32 = jnp.float32

root_two_pi = math.sqrt(2.0 / math.pi)


def gelu_pair(pre):
    inner = root_two_pi * (pre + 0.044715 * pre * pre * pre)
    tangent = jnp.tanh(inner)
    half = 0.5 * (1.0 + tangent)
    slope = half + 0.5 * pre * (1.0 - tangent * tangent) * root_two_pi * (
        1.0 + 3.0 * 0.044715 * pre * pre
    )
    return pre * half, slope


def dot(left, right, over_left, over_right):
    return lax.dot_general(
        left, right, (((over_left,), (over_right,)), ((), ())), preferred_element_type=F32
    )


def iota(shape, dim):
    return lax.broadcasted_iota(jnp.int32, shape, dim)


def params(mib):
    return pltpu.CompilerParams(vmem_limit_bytes=mib * MIB)


def cost(flops, moved):
    return pl.CostEstimate(flops=flops, bytes_accessed=moved, transcendentals=0)


def slot_hits(expert_ref, slot_ref, kept_ref, slots):
    position = jnp.where(kept_ref[...] == 1, expert_ref[...] * CAP + slot_ref[...], -1)
    return iota((slots, position.shape[1]), 0) == position


CARRIED = (0, 5, 2)


def dispatch_kernel(me_ref, expert_ref, slot_ref, kept_ref, gate_ref, tokens, grad_out, send_ref, x_ref, dy_ref, sems):
    rows, half = send_ref.shape
    loads = [
        pltpu.make_async_copy(tokens, x_ref, sems.at[0]),
        pltpu.make_async_copy(grad_out, dy_ref, sems.at[1]),
    ]
    for load in loads:
        load.start()
    position = jnp.where(kept_ref[...] == 1, expert_ref[...] * CAP + slot_ref[...], -1)
    run = half // len(CARRIED)
    row = iota((rows, position.shape[1]), 0)
    hits = [(row & ~7) + ((me_ref[0] + offset) & 7) == position for offset in CARRIED]
    gate_row = gate_ref[...].astype(F32).reshape(1, -1)
    totals = [None] * len(CARRIED)
    for r in range(8):
        ref, factor = ((x_ref, 1.0), (dy_ref, gate_row))[r // 4]
        if r % 4 == 0:
            loads[r // 4].wait()
        piece = ref[:, (r % 4) * run : (r % 4 + 1) * run]
        for k, hit in enumerate(hits):
            pick = jnp.where(hit & ((row & 7) == r), factor, 0.0).astype(BF16)
            term = dot(pick, piece, 1, 0)
            totals[k] = term if r == 0 else totals[k] + term
    for k, total in enumerate(totals):
        send_ref[:, k * run : (k + 1) * run] = total.astype(BF16)


def dispatch(me, slots, index_rows, gate, tokens, grad_out):
    count, width = tokens.shape
    return pl.pallas_call(
        dispatch_kernel,
        out_shape=jax.ShapeDtypeStruct((slots, width // 4 * len(CARRIED)), BF16),
        in_specs=[SMEM] + [VMEM] * 4 + [ANY] * 2,
        out_specs=VMEM,
        scratch_shapes=[
            pltpu.VMEM((count, width), BF16),
            pltpu.VMEM((count, width), BF16),
            pltpu.SemaphoreType.DMA((2,)),
        ],
        compiler_params=params(58),
        cost_estimate=cost(4 * slots * count * width, 5 * slots * width),
    )(me, *index_rows, gate, tokens, grad_out)


def expert_kernel(
    me_ref, data_ref, own, before, after, w_in, w_out, rows, acts, mine,
    own_ref, before_ref, after_ref, x_ref, s_ref, in_ref, out_ref, rows_ref, acts_ref, mine_ref, sems,
):
    slots, width = x_ref.shape
    hidden_width = in_ref.shape[1]
    quarter, part_rows = width // 4, slots // 8
    parts = rows_ref.shape[0]
    loads = [
        pltpu.make_async_copy(own, own_ref, sems.at[0]),
        pltpu.make_async_copy(before, before_ref, sems.at[1]),
        pltpu.make_async_copy(after, after_ref, sems.at[2]),
        pltpu.make_async_copy(w_in, in_ref, sems.at[3]),
        pltpu.make_async_copy(w_out, out_ref, sems.at[4]),
    ]
    for load in loads:
        load.start()
    square = (slots, slots)
    to, at = iota(square, 0), iota(square, 1)
    unpack = jnp.where(at == (to % part_rows) * 8 + to // part_rows, 1.0, 0.0).astype(BF16)
    middle = quarter // 2
    for k, (ref, offset, skip) in enumerate(((own_ref, 0, 0), (before_ref, 7, 0), (after_ref, 1, middle))):
        loads[k].wait()
        plain = dot(unpack, ref[...], 1, 0).astype(BF16)
        for carried, slot_offset in enumerate(CARRIED):
            start = max(carried * quarter, skip)
            end = min((carried + 1) * quarter, skip + ref.shape[1])
            slot = (me_ref[0] + offset + slot_offset) & 7
            place = pl.ds(pl.multiple_of(slot * part_rows, part_rows), part_rows)
            for r in range(8):
                target = (x_ref, s_ref)[r // 4]
                first = (r % 4) * quarter + start - carried * quarter
                target[place, first : first + end - start] = plain[
                    r * part_rows : (r + 1) * part_rows, start - skip : end - skip
                ]
    for k, ref in enumerate((x_ref, x_ref, s_ref, s_ref)):
        for target, mask in ((mine_ref, (0, 2)[k % 2]), (acts_ref, (1, 3)[k % 2])):
            place = pl.ds(pl.multiple_of((data_ref[0] ^ mask) * quarter, quarter), quarter)
            target[:, k * quarter : (k + 1) * quarter] = ref[:, place]
    stores = [
        pltpu.make_async_copy(mine_ref, mine, sems.at[7 + parts]),
        pltpu.make_async_copy(acts_ref, acts, sems.at[8 + parts]),
    ]
    stores[0].start()
    loads[3].wait()
    pre = dot(x_ref[...], in_ref[...], 1, 0)
    value, slope = gelu_pair(pre)
    hidden = value.astype(BF16)
    acts_ref[:, width + hidden_width :] = hidden
    loads[4].wait()
    back = dot(s_ref[...], out_ref[...], 1, 1)
    grad_pre = (back * slope).astype(BF16)
    acts_ref[:, width : width + hidden_width] = grad_pre
    stores[1].start()
    gate = jnp.sum(hidden.astype(F32) * back, axis=1, keepdims=True)
    gate_row = jnp.sum(jnp.where(to == at, gate, 0.0), axis=0, keepdims=True)
    gate_rows = jnp.broadcast_to(gate_row, (16, slots)).astype(BF16)
    block = width // parts
    for part in range(parts):
        term = dot(grad_pre, in_ref[part * block : (part + 1) * block, :], 1, 1)
        rows_ref[part, :slots, :] = term.astype(BF16)
        rows_ref[part, slots:, :] = gate_rows
        stores.append(pltpu.make_async_copy(rows_ref.at[part], rows.at[part], sems.at[7 + part]))
        stores[-1].start()
    for store in stores:
        store.wait()


def expert(me, data, packs, w_in, w_out, parts):
    slots = packs[0].shape[0]
    width, hidden_width = w_in.shape
    outs = (
        (parts, slots + 16, width // parts),
        (slots, width + 2 * hidden_width),
        (slots, width),
    )
    return pl.pallas_call(
        expert_kernel,
        out_shape=tuple(jax.ShapeDtypeStruct(shape, BF16) for shape in outs),
        in_specs=[SMEM, SMEM] + [ANY] * 5,
        out_specs=(ANY, ANY, ANY),
        scratch_shapes=[
            *[pltpu.VMEM(pack.shape, BF16) for pack in packs],
            pltpu.VMEM((slots, width), BF16),
            pltpu.VMEM((slots, width), BF16),
            pltpu.VMEM(w_in.shape, BF16),
            pltpu.VMEM(w_out.shape, BF16),
        ]
        + [pltpu.VMEM(shape, BF16) for shape in outs]
        + [pltpu.SemaphoreType.DMA((9 + parts,))],
        compiler_params=params(59),
        cost_estimate=cost(
            6 * slots * width * hidden_width, 4 * width * (slots + hidden_width) + 8 * slots * width
        ),
    )(me, data, *packs, w_in, w_out)


def sum_kernel(terms_ref, out_ref):
    slots = out_ref.shape[0]
    block = terms_ref.shape[2]
    total = terms_ref[0].astype(F32)
    for part in range(1, terms_ref.shape[0]):
        total = total + terms_ref[part].astype(F32)
    to, at = iota((slots, slots), 0), iota((slots, slots), 1)
    from_row = (to & 7) * (slots // 8) + (to >> 3)
    order = jnp.where(at == from_row, 1.0, 0.0)
    gate = jnp.sum(order * total[slots : slots + 1], axis=1, keepdims=True)
    sums = dot(order.astype(BF16), total[:slots].astype(BF16), 1, 0)
    out_ref[:, :block] = sums.astype(BF16)
    out_ref[:, block:] = jnp.broadcast_to(gate, (slots, LANES)).astype(BF16)


def sum_terms(terms, slots):
    parts, _, block = terms.shape
    return pl.pallas_call(
        sum_kernel,
        out_shape=jax.ShapeDtypeStruct((slots, block + LANES), BF16),
        in_specs=[VMEM],
        out_specs=VMEM,
        compiler_params=params(24),
        cost_estimate=cost(parts * slots * block, 2 * parts * slots * block),
    )(terms)


def finish_kernel(me_ref, expert_ref, slot_ref, kept_ref, gate_ref, home_ref, *refs):
    same_ref, low_ref, high_ref, tokens_ref, gates_ref = refs
    slots, block = home_ref.shape[0], same_ref.shape[1]
    hits = slot_hits(expert_ref, slot_ref, kept_ref, slots)
    column = home_ref[:, block : block + 1].astype(F32)
    picked = jnp.sum(jnp.where(hits, column, 0.0), axis=0, keepdims=True)
    gate_row = gate_ref[...].astype(F32).reshape(1, -1)
    gates_ref[...] = (picked / gate_row).astype(BF16).reshape(-1)
    choose = jnp.where(hits, 1.0, 0.0).T.astype(BF16)
    odd = me_ref[0] & 1

    def store(index, piece):
        place = pl.multiple_of(index * block, block)
        tokens_ref[:, pl.ds(place, block)] = dot(choose, piece, 1, 0).astype(BF16)

    for k in range(4):
        store(2 * k + odd, same_ref[k * slots : (k + 1) * slots, :])
    for k in range(2):
        store(2 * k + 1 - odd, low_ref[k * slots : (k + 1) * slots, :])
        store(2 * k + 5 - odd, high_ref[k * slots : (k + 1) * slots, :])


def finish(me, index_rows, gate, home, pieces, width):
    count = gate.shape[0]
    return pl.pallas_call(
        finish_kernel,
        out_shape=(
            jax.ShapeDtypeStruct((count, width), BF16),
            jax.ShapeDtypeStruct((count,), BF16),
        ),
        in_specs=[SMEM] + [VMEM] * (5 + len(pieces)),
        out_specs=(VMEM, VMEM),
        compiler_params=params(24),
        cost_estimate=cost(2 * count * count * width, 4 * count * width),
    )(me, *index_rows, gate, home, *pieces)


def weight_kernel(turn, mine_ref, acts_ref, other_ref, *refs):
    added, (in_ref, out_ref) = refs[:-2], refs[-2:]
    quarter, width = in_ref.shape
    grads = slice(4 * quarter, 4 * quarter + width)
    hiddens = slice(4 * quarter + width, 4 * quarter + 2 * width)
    x_cols = slice(turn * quarter, (turn + 1) * quarter)
    s_cols = slice((turn + 2) * quarter, (turn + 3) * quarter)
    first = dot(mine_ref[:, x_cols], acts_ref[:, grads], 0, 0)
    first = first + dot(other_ref[:, x_cols], other_ref[:, grads], 0, 0)
    if added:
        first = first + added[0][...].astype(F32)
    in_ref[...] = first.astype(BF16)
    second = dot(acts_ref[:, hiddens], mine_ref[:, s_cols], 0, 0)
    second = second + dot(other_ref[:, hiddens], other_ref[:, s_cols], 0, 0)
    if added:
        second = second + added[1][...].astype(F32)
    out_ref[...] = second.astype(BF16)


def weight_terms(turn, mine, acts, other, added=()):
    slots = mine.shape[0]
    quarter = mine.shape[1] // 4
    width = (acts.shape[1] - 4 * quarter) // 2
    return pl.pallas_call(
        functools.partial(weight_kernel, turn),
        in_specs=[VMEM] * (3 + len(added)),
        out_specs=(VMEM, VMEM),
        out_shape=(
            jax.ShapeDtypeStruct((quarter, width), BF16),
            jax.ShapeDtypeStruct((width, quarter), BF16),
        ),
        compiler_params=params(24),
        cost_estimate=cost(8 * slots * quarter * width, 8 * slots * (quarter + width) + 4 * quarter * width),
    )(mine, acts, other, *added)


def shift(value, step):
    return lax.ppermute(value, "mp", [(i, (i + step) % 8) for i in range(8)])


def swap(value, bit):
    return lax.ppermute(value, "dp", [(i, i ^ bit) for i in range(4)])


def gather_pieces(piece):
    same = lax.all_gather(
        piece, "mp", axis=0, tiled=True, axis_index_groups=[[0, 2, 4, 6], [1, 3, 5, 7]]
    )
    half = same.shape[0] // 2
    return same, shift(same[:half], 1), shift(same[half:], -1)


def scatter(value, axis):
    return lax.all_to_all(value, axis, split_axis=0, concat_axis=0, tiled=True)


def local(grad_out, tokens, gate, expert_index, slot, kept, w_in, w_out):
    experts = lax.axis_size("expert")
    parts = lax.axis_size("mp")
    count, width = tokens.shape
    slots = experts * CAP
    index_rows = [value.reshape(1, count) for value in (expert_index, slot, kept)]
    me = lax.axis_index("mp").astype(jnp.int32).reshape(1)
    data = lax.axis_index("dp").astype(jnp.int32).reshape(1)

    send = dispatch(me, slots, index_rows, gate, tokens, grad_out)
    came = scatter(send.reshape(experts, CAP, send.shape[1]), "expert").reshape(send.shape)
    middle = width // 8
    packs = (came, shift(came[:, : came.shape[1] - middle], 1), shift(came[:, middle:], -1))
    rows, acts, mine = expert(me, data, packs, w_in[0], w_out[0], parts)
    terms = scatter(rows, "mp")

    other = swap(acts, 1)
    added = [swap(value, 2) for value in weight_terms(1, mine, acts, other)]

    total = sum_terms(terms, slots)
    home = scatter(total.reshape(experts, CAP, total.shape[1]), "expert").reshape(total.shape)
    home, added = lax.optimization_barrier((home, added))
    grad_w_in, grad_w_out = weight_terms(0, mine, acts, other, added)
    pieces = gather_pieces(home[:, : width // parts])
    grad_tokens, grad_gate = finish(me, index_rows, gate, home, pieces, width)
    return (grad_tokens, grad_gate, grad_w_in[None], grad_w_out[None])


def solution(mesh):
    placed = (
        P(("expert", "dp"), None),
        P(("expert", "dp"), None),
        P(("expert", "dp")),
        P(("expert", "dp")),
        P(("expert", "dp")),
        P(("expert", "dp")),
        P("expert", None, "mp"),
        P("expert", "mp", None),
    )
    return jax.shard_map(
        local,
        mesh=mesh,
        in_specs=placed,
        out_specs=(
            P(("expert", "dp"), None),
            P(("expert", "dp")),
            P("expert", "dp", "mp"),
            P("expert", "mp", "dp"),
        ),
        check_vma=False,
    )
```

```python
import functools
import math

import jax
import jax.numpy as jnp
from jax import lax
from jax.experimental import pallas as pl
from jax.experimental.pallas import tpu as pltpu
from jax.sharding import PartitionSpec as P

CAP = 8
LANES = 128
MIB = 1 << 20
VMEM = pl.BlockSpec(memory_space=pltpu.VMEM)
ANY = pl.BlockSpec(memory_space=pl.ANY)
SMEM = pl.BlockSpec(memory_space=pltpu.SMEM)
BF16 = jnp.bfloat16
F32 = jnp.float32

root_two_pi = math.sqrt(2.0 / math.pi)


def gelu_pair(pre):
    inner = root_two_pi * (pre + 0.044715 * pre * pre * pre)
    tangent = jnp.tanh(inner)
    half = 0.5 * (1.0 + tangent)
    slope = half + 0.5 * pre * (1.0 - tangent * tangent) * root_two_pi * (
        1.0 + 3.0 * 0.044715 * pre * pre
    )
    return pre * half, slope


def dot(left, right, over_left, over_right):
    return lax.dot_general(
        left, right, (((over_left,), (over_right,)), ((), ())), preferred_element_type=F32
    )


def iota(shape, dim):
    return lax.broadcasted_iota(jnp.int32, shape, dim)


def params(mib):
    return pltpu.CompilerParams(vmem_limit_bytes=mib * MIB)


def cost(flops, moved):
    return pl.CostEstimate(flops=flops, bytes_accessed=moved, transcendentals=0)


def slot_hits(expert_ref, slot_ref, kept_ref, slots):
    position = jnp.where(kept_ref[...] == 1, expert_ref[...] * CAP + slot_ref[...], -1)
    return iota((slots, position.shape[1]), 0) == position


CARRIED = (0, 5, 2)


def dispatch_kernel(me_ref, expert_ref, slot_ref, kept_ref, gate_ref, tokens, grad_out, send_ref, x_ref, dy_ref, spread_ref, sems):
    rows, half = send_ref.shape
    loads = [
        pltpu.make_async_copy(tokens, x_ref, sems.at[0]),
        pltpu.make_async_copy(grad_out, dy_ref, sems.at[1]),
    ]
    for load in loads:
        load.start()
    position = jnp.where(kept_ref[...] == 1, expert_ref[...] * CAP + slot_ref[...], -1)
    run = half // len(CARRIED)
    experts = rows // 8
    tile = spread_ref.shape[2]
    tiles = run // tile
    gate_row = gate_ref[...].astype(F32).reshape(1, -1)
    row = iota((len(CARRIED) * experts, position.shape[1]), 0)
    carried = row // experts
    offset = jnp.where(carried == 0, CARRIED[0], jnp.where(carried == 1, CARRIED[1], CARRIED[2]))
    hits = (row - carried * experts) * CAP + ((me_ref[0] + offset) & 7) == position
    for side, (ref, factor) in enumerate(((x_ref, 1.0), (dy_ref, gate_row))):
        pick = jnp.where(hits, factor, 0.0).astype(BF16)
        loads[side].wait()
        for part in range(4):
            r = 4 * side + part
            found = dot(pick, ref[:, part * run : (part + 1) * run], 1, 0)
            for k in range(len(CARRIED)):
                for j in range(tiles):
                    term = found[k * experts : (k + 1) * experts, j * tile : (j + 1) * tile]
                    spread_ref[k * tiles + j, pl.ds(r, experts, stride=8), :] = term
    for j in range(spread_ref.shape[0]):
        send_ref[:, j * tile : (j + 1) * tile] = spread_ref[j].astype(BF16)


def dispatch(me, slots, index_rows, gate, tokens, grad_out):
    count, width = tokens.shape
    tile = min(LANES, width // 4)
    return pl.pallas_call(
        dispatch_kernel,
        out_shape=jax.ShapeDtypeStruct((slots, width // 4 * len(CARRIED)), BF16),
        in_specs=[SMEM] + [VMEM] * 4 + [ANY] * 2,
        out_specs=VMEM,
        scratch_shapes=[
            pltpu.VMEM((count, width), BF16),
            pltpu.VMEM((count, width), BF16),
            pltpu.VMEM((width // 4 * len(CARRIED) // tile, slots, tile), F32),
            pltpu.SemaphoreType.DMA((2,)),
        ],
        compiler_params=params(58),
        cost_estimate=cost(4 * slots * count * width, 5 * slots * width),
    )(me, *index_rows, gate, tokens, grad_out)


def expert_kernel(
    me_ref, data_ref, own, before, after, w_in, w_out, rows, acts, mine,
    own_ref, before_ref, after_ref, x_ref, s_ref, in_ref, out_ref, rows_ref, acts_ref, mine_ref, sems,
):
    slots, width = x_ref.shape
    hidden_width = in_ref.shape[1]
    quarter, part_rows = width // 4, slots // 8
    parts = rows_ref.shape[0]
    loads = [
        pltpu.make_async_copy(own, own_ref, sems.at[0]),
        pltpu.make_async_copy(before, before_ref, sems.at[1]),
        pltpu.make_async_copy(after, after_ref, sems.at[2]),
        pltpu.make_async_copy(w_in, in_ref, sems.at[3]),
        pltpu.make_async_copy(w_out, out_ref, sems.at[4]),
    ]
    for load in loads:
        load.start()
    square = (slots, slots)
    to, at = iota(square, 0), iota(square, 1)
    unpack = jnp.where(at == (to % part_rows) * 8 + to // part_rows, 1.0, 0.0).astype(BF16)
    middle = quarter // 2
    for k, (ref, offset, skip) in enumerate(((own_ref, 0, 0), (before_ref, 7, 0), (after_ref, 1, middle))):
        loads[k].wait()
        plain = dot(unpack, ref[...], 1, 0).astype(BF16)
        for carried, slot_offset in enumerate(CARRIED):
            start = max(carried * quarter, skip)
            end = min((carried + 1) * quarter, skip + ref.shape[1])
            slot = (me_ref[0] + offset + slot_offset) & 7
            place = pl.ds(pl.multiple_of(slot * part_rows, part_rows), part_rows)
            for r in range(8):
                target = (x_ref, s_ref)[r // 4]
                first = (r % 4) * quarter + start - carried * quarter
                target[place, first : first + end - start] = plain[
                    r * part_rows : (r + 1) * part_rows, start - skip : end - skip
                ]
    for k, ref in enumerate((x_ref, x_ref, s_ref, s_ref)):
        for target, mask in ((mine_ref, (0, 2)[k % 2]), (acts_ref, (1, 3)[k % 2])):
            place = pl.ds(pl.multiple_of((data_ref[0] ^ mask) * quarter, quarter), quarter)
            target[:, k * quarter : (k + 1) * quarter] = ref[:, place]
    stores = [
        pltpu.make_async_copy(mine_ref, mine, sems.at[7 + parts]),
        pltpu.make_async_copy(acts_ref, acts, sems.at[8 + parts]),
    ]
    stores[0].start()
    loads[3].wait()
    pre = dot(x_ref[...], in_ref[...], 1, 0)
    loads[4].wait()
    back = dot(s_ref[...], out_ref[...], 1, 1)
    value, slope = gelu_pair(pre)
    hidden = value.astype(BF16)
    acts_ref[:, width + hidden_width :] = hidden
    grad_pre = (back * slope).astype(BF16)
    acts_ref[:, width : width + hidden_width] = grad_pre
    stores[1].start()
    gate = jnp.sum(hidden.astype(F32) * back, axis=1, keepdims=True)
    gate_row = jnp.sum(jnp.where(to == at, gate, 0.0), axis=0, keepdims=True)
    gate_rows = jnp.broadcast_to(gate_row, (16, slots)).astype(BF16)
    block = width // parts
    for part in range(parts):
        term = dot(grad_pre, in_ref[part * block : (part + 1) * block, :], 1, 1)
        rows_ref[part, :slots, :] = term.astype(BF16)
        rows_ref[part, slots:, :] = gate_rows
        stores.append(pltpu.make_async_copy(rows_ref.at[part], rows.at[part], sems.at[7 + part]))
        stores[-1].start()
    for store in stores:
        store.wait()


def expert(me, data, packs, w_in, w_out, parts):
    slots = packs[0].shape[0]
    width, hidden_width = w_in.shape
    outs = (
        (parts, slots + 16, width // parts),
        (slots, width + 2 * hidden_width),
        (slots, width),
    )
    return pl.pallas_call(
        expert_kernel,
        out_shape=tuple(jax.ShapeDtypeStruct(shape, BF16) for shape in outs),
        in_specs=[SMEM, SMEM] + [ANY] * 5,
        out_specs=(ANY, ANY, ANY),
        scratch_shapes=[
            *[pltpu.VMEM(pack.shape, BF16) for pack in packs],
            pltpu.VMEM((slots, width), BF16),
            pltpu.VMEM((slots, width), BF16),
            pltpu.VMEM(w_in.shape, BF16),
            pltpu.VMEM(w_out.shape, BF16),
        ]
        + [pltpu.VMEM(shape, BF16) for shape in outs]
        + [pltpu.SemaphoreType.DMA((9 + parts,))],
        compiler_params=params(52),
        cost_estimate=cost(
            6 * slots * width * hidden_width, 4 * width * (slots + hidden_width) + 8 * slots * width
        ),
    )(me, data, *packs, w_in, w_out)


def sum_kernel(terms_ref, out_ref):
    slots = out_ref.shape[0]
    block = terms_ref.shape[2]
    total = terms_ref[0].astype(F32)
    for part in range(1, terms_ref.shape[0]):
        total = total + terms_ref[part].astype(F32)
    to, at = iota((slots, slots), 0), iota((slots, slots), 1)
    from_row = (to & 7) * (slots // 8) + (to >> 3)
    order = jnp.where(at == from_row, 1.0, 0.0)
    gate = jnp.sum(order * total[slots : slots + 1], axis=1, keepdims=True)
    sums = dot(order.astype(BF16), total[:slots].astype(BF16), 1, 0)
    out_ref[:, :block] = sums.astype(BF16)
    out_ref[:, block:] = jnp.broadcast_to(gate, (slots, LANES)).astype(BF16)


def sum_terms(terms, slots):
    parts, _, block = terms.shape
    return pl.pallas_call(
        sum_kernel,
        out_shape=jax.ShapeDtypeStruct((slots, block + LANES), BF16),
        in_specs=[VMEM],
        out_specs=VMEM,
        compiler_params=params(24),
        cost_estimate=cost(parts * slots * block, 2 * parts * slots * block),
    )(terms)


def finish_kernel(me_ref, expert_ref, slot_ref, kept_ref, gate_ref, home_ref, *refs):
    same_ref, low_ref, high_ref, tokens_ref, gates_ref = refs
    slots, block = home_ref.shape[0], same_ref.shape[1]
    hits = slot_hits(expert_ref, slot_ref, kept_ref, slots)
    column = home_ref[:, block : block + 1].astype(F32)
    picked = jnp.sum(jnp.where(hits, column, 0.0), axis=0, keepdims=True)
    gate_row = gate_ref[...].astype(F32).reshape(1, -1)
    gates_ref[...] = (picked / gate_row).astype(BF16).reshape(-1)
    choose = jnp.where(hits, 1.0, 0.0).T.astype(BF16)
    odd = me_ref[0] & 1

    def store(index, piece):
        place = pl.multiple_of(index * block, block)
        tokens_ref[:, pl.ds(place, block)] = dot(choose, piece, 1, 0).astype(BF16)

    for k in range(4):
        store(2 * k + odd, same_ref[k * slots : (k + 1) * slots, :])
    for k in range(2):
        store(2 * k + 1 - odd, low_ref[k * slots : (k + 1) * slots, :])
        store(2 * k + 5 - odd, high_ref[k * slots : (k + 1) * slots, :])


def finish(me, index_rows, gate, home, pieces, width):
    count = gate.shape[0]
    return pl.pallas_call(
        finish_kernel,
        out_shape=(
            jax.ShapeDtypeStruct((count, width), BF16),
            jax.ShapeDtypeStruct((count,), BF16),
        ),
        in_specs=[SMEM] + [VMEM] * (5 + len(pieces)),
        out_specs=(VMEM, VMEM),
        compiler_params=params(24),
        cost_estimate=cost(2 * count * count * width, 4 * count * width),
    )(me, *index_rows, gate, home, *pieces)


def weight_kernel(turn, mine_ref, acts_ref, other_ref, *refs):
    added, (in_ref, out_ref) = refs[:-2], refs[-2:]
    quarter, width = in_ref.shape
    grads = slice(4 * quarter, 4 * quarter + width)
    hiddens = slice(4 * quarter + width, 4 * quarter + 2 * width)
    x_cols = slice(turn * quarter, (turn + 1) * quarter)
    s_cols = slice((turn + 2) * quarter, (turn + 3) * quarter)
    first = dot(mine_ref[:, x_cols], acts_ref[:, grads], 0, 0)
    first = first + dot(other_ref[:, x_cols], other_ref[:, grads], 0, 0)
    if added:
        first = first + added[0][...].astype(F32)
    in_ref[...] = first.astype(BF16)
    second = dot(acts_ref[:, hiddens], mine_ref[:, s_cols], 0, 0)
    second = second + dot(other_ref[:, hiddens], other_ref[:, s_cols], 0, 0)
    if added:
        second = second + added[1][...].astype(F32)
    out_ref[...] = second.astype(BF16)


def weight_terms(turn, mine, acts, other, added=()):
    slots = mine.shape[0]
    quarter = mine.shape[1] // 4
    width = (acts.shape[1] - 4 * quarter) // 2
    return pl.pallas_call(
        functools.partial(weight_kernel, turn),
        in_specs=[VMEM] * (3 + len(added)),
        out_specs=(VMEM, VMEM),
        out_shape=(
            jax.ShapeDtypeStruct((quarter, width), BF16),
            jax.ShapeDtypeStruct((width, quarter), BF16),
        ),
        compiler_params=params(24),
        cost_estimate=cost(8 * slots * quarter * width, 8 * slots * (quarter + width) + 4 * quarter * width),
    )(mine, acts, other, *added)


def shift(value, step):
    return lax.ppermute(value, "mp", [(i, (i + step) % 8) for i in range(8)])


def swap(value, bit):
    return lax.ppermute(value, "dp", [(i, i ^ bit) for i in range(4)])


def gather_pieces(piece):
    same = lax.all_gather(
        piece, "mp", axis=0, tiled=True, axis_index_groups=[[0, 2, 4, 6], [1, 3, 5, 7]]
    )
    half = same.shape[0] // 2
    return same, shift(same[:half], 1), shift(same[half:], -1)


def scatter(value, axis):
    return lax.all_to_all(value, axis, split_axis=0, concat_axis=0, tiled=True)


def local(grad_out, tokens, gate, expert_index, slot, kept, w_in, w_out):
    experts = lax.axis_size("expert")
    parts = lax.axis_size("mp")
    count, width = tokens.shape
    slots = experts * CAP
    index_rows = [value.reshape(1, count) for value in (expert_index, slot, kept)]
    me = lax.axis_index("mp").astype(jnp.int32).reshape(1)
    data = lax.axis_index("dp").astype(jnp.int32).reshape(1)

    send = dispatch(me, slots, index_rows, gate, tokens, grad_out)
    came = scatter(send.reshape(experts, CAP, send.shape[1]), "expert").reshape(send.shape)
    middle = width // 8
    packs = (came, shift(came[:, : came.shape[1] - middle], 1), shift(came[:, middle:], -1))
    rows, acts, mine = expert(me, data, packs, w_in[0], w_out[0], parts)
    terms = scatter(rows, "mp")

    other = swap(acts, 1)
    added = [swap(value, 2) for value in weight_terms(1, mine, acts, other)]

    total = sum_terms(terms, slots)
    home = scatter(total.reshape(experts, CAP, total.shape[1]), "expert").reshape(total.shape)
    home, added = lax.optimization_barrier((home, added))
    grad_w_in, grad_w_out = weight_terms(0, mine, acts, other, added)
    pieces = gather_pieces(home[:, : width // parts])
    grad_tokens, grad_gate = finish(me, index_rows, gate, home, pieces, width)
    return (grad_tokens, grad_gate, grad_w_in[None], grad_w_out[None])


def solution(mesh):
    placed = (
        P(("expert", "dp"), None),
        P(("expert", "dp"), None),
        P(("expert", "dp")),
        P(("expert", "dp")),
        P(("expert", "dp")),
        P(("expert", "dp")),
        P("expert", None, "mp"),
        P("expert", "mp", None),
    )
    return jax.shard_map(
        local,
        mesh=mesh,
        in_specs=placed,
        out_specs=(
            P(("expert", "dp"), None),
            P(("expert", "dp")),
            P("expert", "dp", "mp"),
            P("expert", "mp", "dp"),
        ),
        check_vma=False,
    )
```

```python
import functools
import math

import jax
import jax.numpy as jnp
from jax import lax
from jax.experimental import pallas as pl
from jax.experimental.pallas import tpu as pltpu
from jax.sharding import PartitionSpec as P

CAP = 8
LANES = 128
MIB = 1 << 20
VMEM = pl.BlockSpec(memory_space=pltpu.VMEM)
ANY = pl.BlockSpec(memory_space=pl.ANY)
SMEM = pl.BlockSpec(memory_space=pltpu.SMEM)
BF16 = jnp.bfloat16
F32 = jnp.float32

root_two_pi = math.sqrt(2.0 / math.pi)


def gelu_pair(pre):
    inner = root_two_pi * (pre + 0.044715 * pre * pre * pre)
    tangent = jnp.tanh(inner)
    half = 0.5 * (1.0 + tangent)
    slope = half + 0.5 * pre * (1.0 - tangent * tangent) * root_two_pi * (
        1.0 + 3.0 * 0.044715 * pre * pre
    )
    return pre * half, slope


def dot(left, right, over_left, over_right):
    return lax.dot_general(
        left, right, (((over_left,), (over_right,)), ((), ())), preferred_element_type=F32
    )


def iota(shape, dim):
    return lax.broadcasted_iota(jnp.int32, shape, dim)


def params(mib):
    return pltpu.CompilerParams(vmem_limit_bytes=mib * MIB)


def cost(flops, moved):
    return pl.CostEstimate(flops=flops, bytes_accessed=moved, transcendentals=0)


def slot_hits(expert_ref, slot_ref, kept_ref, slots):
    position = jnp.where(kept_ref[...] == 1, expert_ref[...] * CAP + slot_ref[...], -1)
    return iota((slots, position.shape[1]), 0) == position


CARRIED = (0, 5, 2)


def dispatch_kernel(me_ref, expert_ref, slot_ref, kept_ref, gate_ref, tokens, grad_out, send_ref, x_ref, dy_ref, spread_ref, sems):
    rows, half = send_ref.shape
    loads = [
        pltpu.make_async_copy(tokens, x_ref, sems.at[0]),
        pltpu.make_async_copy(grad_out, dy_ref, sems.at[1]),
    ]
    for load in loads:
        load.start()
    position = jnp.where(kept_ref[...] == 1, expert_ref[...] * CAP + slot_ref[...], -1)
    run = half // len(CARRIED)
    experts = rows // 8
    tile = spread_ref.shape[2]
    tiles = run // tile
    gate_row = gate_ref[...].astype(F32).reshape(1, -1)
    row = iota((len(CARRIED) * experts, position.shape[1]), 0)
    carried = row // experts
    offset = jnp.where(carried == 0, CARRIED[0], jnp.where(carried == 1, CARRIED[1], CARRIED[2]))
    hits = (row - carried * experts) * CAP + ((me_ref[0] + offset) & 7) == position
    for side, (ref, factor) in enumerate(((x_ref, 1.0), (dy_ref, gate_row))):
        pick = jnp.where(hits, factor, 0.0).astype(BF16)
        loads[side].wait()
        for part in range(4):
            r = 4 * side + part
            found = dot(pick, ref[:, part * run : (part + 1) * run], 1, 0)
            for k in range(len(CARRIED)):
                for j in range(tiles):
                    term = found[k * experts : (k + 1) * experts, j * tile : (j + 1) * tile]
                    spread_ref[k * tiles + j, pl.ds(r, experts, stride=8), :] = term
    for j in range(spread_ref.shape[0]):
        send_ref[:, j * tile : (j + 1) * tile] = spread_ref[j].astype(BF16)


def dispatch(me, slots, index_rows, gate, tokens, grad_out):
    count, width = tokens.shape
    tile = min(LANES, width // 4)
    return pl.pallas_call(
        dispatch_kernel,
        out_shape=jax.ShapeDtypeStruct((slots, width // 4 * len(CARRIED)), BF16),
        in_specs=[SMEM] + [VMEM] * 4 + [ANY] * 2,
        out_specs=VMEM,
        scratch_shapes=[
            pltpu.VMEM((count, width), BF16),
            pltpu.VMEM((count, width), BF16),
            pltpu.VMEM((width // 4 * len(CARRIED) // tile, slots, tile), F32),
            pltpu.SemaphoreType.DMA((2,)),
        ],
        compiler_params=params(58),
        cost_estimate=cost(4 * slots * count * width, 5 * slots * width),
    )(me, *index_rows, gate, tokens, grad_out)


def expert_kernel(
    me_ref, data_ref, own, before, after, w_in, w_out, rows, acts, mine,
    own_ref, before_ref, after_ref, x_ref, s_ref, in_ref, out_ref, rows_ref, acts_ref, mine_ref, sems,
):
    slots, width = x_ref.shape
    hidden_width = in_ref.shape[1]
    quarter, part_rows = width // 4, slots // 8
    parts = rows_ref.shape[0]
    loads = [
        pltpu.make_async_copy(own, own_ref, sems.at[0]),
        pltpu.make_async_copy(before, before_ref, sems.at[1]),
        pltpu.make_async_copy(after, after_ref, sems.at[2]),
        pltpu.make_async_copy(w_in, in_ref, sems.at[3]),
        pltpu.make_async_copy(w_out, out_ref, sems.at[4]),
    ]
    for load in loads:
        load.start()
    square = (slots, slots)
    to, at = iota(square, 0), iota(square, 1)
    unpack = jnp.where(at == (to % part_rows) * 8 + to // part_rows, 1.0, 0.0).astype(BF16)
    middle = quarter // 2
    for k, (ref, offset, skip) in enumerate(((own_ref, 0, 0), (before_ref, 7, 0), (after_ref, 1, middle))):
        loads[k].wait()
        plain = dot(unpack, ref[...], 1, 0).astype(BF16)
        for carried, slot_offset in enumerate(CARRIED):
            start = max(carried * quarter, skip)
            end = min((carried + 1) * quarter, skip + ref.shape[1])
            slot = (me_ref[0] + offset + slot_offset) & 7
            place = pl.ds(pl.multiple_of(slot * part_rows, part_rows), part_rows)
            for r in range(8):
                target = (x_ref, s_ref)[r // 4]
                first = (r % 4) * quarter + start - carried * quarter
                target[place, first : first + end - start] = plain[
                    r * part_rows : (r + 1) * part_rows, start - skip : end - skip
                ]
    for k, ref in enumerate((x_ref, x_ref, s_ref, s_ref)):
        for target, mask in ((mine_ref, (0, 2)[k % 2]), (acts_ref, (1, 3)[k % 2])):
            place = pl.ds(pl.multiple_of((data_ref[0] ^ mask) * quarter, quarter), quarter)
            target[:, k * quarter : (k + 1) * quarter] = ref[:, place]
    stores = [
        pltpu.make_async_copy(mine_ref, mine, sems.at[7 + parts]),
        pltpu.make_async_copy(acts_ref, acts, sems.at[8 + parts]),
    ]
    stores[0].start()
    loads[3].wait()
    pre = dot(x_ref[...], in_ref[...], 1, 0)
    loads[4].wait()
    back = dot(s_ref[...], out_ref[...], 1, 1)
    value, slope = gelu_pair(pre)
    hidden = value.astype(BF16)
    acts_ref[:, width + hidden_width :] = hidden
    grad_pre = (back * slope).astype(BF16)
    acts_ref[:, width : width + hidden_width] = grad_pre
    stores[1].start()
    gate = jnp.sum(hidden.astype(F32) * back, axis=1, keepdims=True)
    gate_row = jnp.sum(jnp.where(to == at, gate, 0.0), axis=0, keepdims=True)
    gate_rows = jnp.broadcast_to(gate_row, (16, slots)).astype(BF16)
    block = width // parts
    for part in range(parts):
        term = dot(grad_pre, in_ref[part * block : (part + 1) * block, :], 1, 1)
        rows_ref[part, :slots, :] = term.astype(BF16)
        rows_ref[part, slots:, :] = gate_rows
        stores.append(pltpu.make_async_copy(rows_ref.at[part], rows.at[part], sems.at[7 + part]))
        stores[-1].start()
    for store in stores:
        store.wait()


def expert(me, data, packs, w_in, w_out, parts):
    slots = packs[0].shape[0]
    width, hidden_width = w_in.shape
    outs = (
        (parts, slots + 16, width // parts),
        (slots, width + 2 * hidden_width),
        (slots, width),
    )
    return pl.pallas_call(
        expert_kernel,
        out_shape=tuple(jax.ShapeDtypeStruct(shape, BF16) for shape in outs),
        in_specs=[SMEM, SMEM] + [ANY] * 5,
        out_specs=(ANY, ANY, ANY),
        scratch_shapes=[
            *[pltpu.VMEM(pack.shape, BF16) for pack in packs],
            pltpu.VMEM((slots, width), BF16),
            pltpu.VMEM((slots, width), BF16),
            pltpu.VMEM(w_in.shape, BF16),
            pltpu.VMEM(w_out.shape, BF16),
        ]
        + [pltpu.VMEM(shape, BF16) for shape in outs]
        + [pltpu.SemaphoreType.DMA((9 + parts,))],
        compiler_params=params(52),
        cost_estimate=cost(
            6 * slots * width * hidden_width, 4 * width * (slots + hidden_width) + 8 * slots * width
        ),
    )(me, data, *packs, w_in, w_out)


def sum_kernel(terms_ref, out_ref):
    slots = out_ref.shape[0]
    block = terms_ref.shape[2]
    total = terms_ref[0].astype(F32)
    for part in range(1, terms_ref.shape[0]):
        total = total + terms_ref[part].astype(F32)
    to, at = iota((slots, slots), 0), iota((slots, slots), 1)
    from_row = (to & 7) * (slots // 8) + (to >> 3)
    order = jnp.where(at == from_row, 1.0, 0.0)
    gate = jnp.sum(order * total[slots : slots + 1], axis=1, keepdims=True)
    sums = dot(order.astype(BF16), total[:slots].astype(BF16), 1, 0)
    out_ref[:, :block] = sums.astype(BF16)
    out_ref[:, block:] = jnp.broadcast_to(gate, (slots, LANES)).astype(BF16)


def sum_terms(terms, slots):
    parts, _, block = terms.shape
    return pl.pallas_call(
        sum_kernel,
        out_shape=jax.ShapeDtypeStruct((slots, block + LANES), BF16),
        in_specs=[VMEM],
        out_specs=VMEM,
        compiler_params=params(24),
        cost_estimate=cost(parts * slots * block, 2 * parts * slots * block),
    )(terms)


def finish_kernel(me_ref, expert_ref, slot_ref, kept_ref, gate_ref, home_ref, *refs):
    same_ref, low_ref, high_ref, tokens_ref, gates_ref = refs
    slots, block = home_ref.shape[0], same_ref.shape[1]
    hits = slot_hits(expert_ref, slot_ref, kept_ref, slots)
    column = home_ref[:, block : block + 1].astype(F32)
    picked = jnp.sum(jnp.where(hits, column, 0.0), axis=0, keepdims=True)
    gate_row = gate_ref[...].astype(F32).reshape(1, -1)
    gates_ref[...] = (picked / gate_row).astype(BF16).reshape(-1)
    choose = jnp.where(hits, 1.0, 0.0).T.astype(BF16)
    odd = me_ref[0] & 1

    def store(index, piece):
        place = pl.multiple_of(index * block, block)
        tokens_ref[:, pl.ds(place, block)] = dot(choose, piece, 1, 0).astype(BF16)

    for k in range(4):
        store(2 * k + odd, same_ref[k * slots : (k + 1) * slots, :])
    for k in range(2):
        store(2 * k + 1 - odd, low_ref[k * slots : (k + 1) * slots, :])
        store(2 * k + 5 - odd, high_ref[k * slots : (k + 1) * slots, :])


def finish(me, index_rows, gate, home, pieces, width):
    count = gate.shape[0]
    return pl.pallas_call(
        finish_kernel,
        out_shape=(
            jax.ShapeDtypeStruct((count, width), BF16),
            jax.ShapeDtypeStruct((count,), BF16),
        ),
        in_specs=[SMEM] + [VMEM] * (5 + len(pieces)),
        out_specs=(VMEM, VMEM),
        compiler_params=params(24),
        cost_estimate=cost(2 * count * count * width, 4 * count * width),
    )(me, *index_rows, gate, home, *pieces)


def term(left, mine_ref, acts_ref, other_ref, turn, first, activations):
    quarter = mine_ref.shape[1] // 4
    cols = slice((turn + first) * quarter, (turn + first + 1) * quarter)
    total = None
    for rows_ref, from_ref in ((mine_ref, acts_ref), (other_ref, other_ref)):
        pair = rows_ref[:, cols], from_ref[:, activations]
        product = dot(*(pair if left else pair[::-1]), 0, 0)
        total = product if total is None else total + product
    return total


def pass_kernel(mine_ref, acts_ref, other_ref, out_ref):
    quarter, width = mine_ref.shape[1] // 4, out_ref.shape[1]
    grads = slice(4 * quarter, 4 * quarter + width)
    hiddens = slice(4 * quarter + width, 4 * quarter + 2 * width)
    out_ref[:quarter] = term(True, mine_ref, acts_ref, other_ref, 1, 0, grads).astype(BF16)
    out_ref[quarter:] = term(True, mine_ref, acts_ref, other_ref, 1, 2, hiddens).astype(BF16)


def keep_kernel(mine_ref, acts_ref, other_ref, added_ref, in_ref, out_ref):
    quarter, width = in_ref.shape
    grads = slice(4 * quarter, 4 * quarter + width)
    hiddens = slice(4 * quarter + width, 4 * quarter + 2 * width)
    first = term(True, mine_ref, acts_ref, other_ref, 0, 0, grads)
    in_ref[...] = (first + added_ref[:quarter].astype(F32)).astype(BF16)
    second = term(False, mine_ref, acts_ref, other_ref, 0, 2, hiddens)
    out_ref[...] = (second + added_ref[quarter:].astype(F32).T).astype(BF16)


def weight_terms(mine, acts, other, added=None):
    slots = mine.shape[0]
    quarter = mine.shape[1] // 4
    width = (acts.shape[1] - 4 * quarter) // 2
    shapes = ((2 * quarter, width),) if added is None else ((quarter, width), (width, quarter))
    args = (mine, acts, other) if added is None else (mine, acts, other, added)
    return pl.pallas_call(
        pass_kernel if added is None else keep_kernel,
        in_specs=[VMEM] * len(args),
        out_specs=(VMEM,) * len(shapes),
        out_shape=tuple(jax.ShapeDtypeStruct(shape, BF16) for shape in shapes),
        compiler_params=params(24 if added is None else 24),
        cost_estimate=cost(8 * slots * quarter * width, 8 * slots * (quarter + width) + 4 * quarter * width),
    )(*args)


def shift(value, step):
    return lax.ppermute(value, "mp", [(i, (i + step) % 8) for i in range(8)])


def swap(value, bit):
    return lax.ppermute(value, "dp", [(i, i ^ bit) for i in range(4)])


def gather_pieces(piece):
    same = lax.all_gather(
        piece, "mp", axis=0, tiled=True, axis_index_groups=[[0, 2, 4, 6], [1, 3, 5, 7]]
    )
    half = same.shape[0] // 2
    return same, shift(same[:half], 1), shift(same[half:], -1)


def scatter(value, axis):
    return lax.all_to_all(value, axis, split_axis=0, concat_axis=0, tiled=True)


def local(grad_out, tokens, gate, expert_index, slot, kept, w_in, w_out):
    experts = lax.axis_size("expert")
    parts = lax.axis_size("mp")
    count, width = tokens.shape
    slots = experts * CAP
    index_rows = [value.reshape(1, count) for value in (expert_index, slot, kept)]
    me = lax.axis_index("mp").astype(jnp.int32).reshape(1)
    data = lax.axis_index("dp").astype(jnp.int32).reshape(1)

    send = dispatch(me, slots, index_rows, gate, tokens, grad_out)
    came = scatter(send.reshape(experts, CAP, send.shape[1]), "expert").reshape(send.shape)
    middle = width // 8
    packs = (came, shift(came[:, : came.shape[1] - middle], 1), shift(came[:, middle:], -1))
    rows, acts, mine = expert(me, data, packs, w_in[0], w_out[0], parts)
    terms = scatter(rows, "mp")

    other = swap(acts, 1)
    added = swap(weight_terms(mine, acts, other)[0], 2)

    total = sum_terms(terms, slots)
    home = scatter(total.reshape(experts, CAP, total.shape[1]), "expert").reshape(total.shape)
    home, added = lax.optimization_barrier((home, added))
    grad_w_in, grad_w_out = weight_terms(mine, acts, other, added)
    pieces = gather_pieces(home[:, : width // parts])
    grad_tokens, grad_gate = finish(me, index_rows, gate, home, pieces, width)
    return (grad_tokens, grad_gate, grad_w_in[None], grad_w_out[None])


def solution(mesh):
    placed = (
        P(("expert", "dp"), None),
        P(("expert", "dp"), None),
        P(("expert", "dp")),
        P(("expert", "dp")),
        P(("expert", "dp")),
        P(("expert", "dp")),
        P("expert", None, "mp"),
        P("expert", "mp", None),
    )
    return jax.shard_map(
        local,
        mesh=mesh,
        in_specs=placed,
        out_specs=(
            P(("expert", "dp"), None),
            P(("expert", "dp")),
            P("expert", "dp", "mp"),
            P("expert", "mp", "dp"),
        ),
        check_vma=False,
    )
```

```python
import functools
import math

import jax
import jax.numpy as jnp
from jax import lax
from jax.experimental import pallas as pl
from jax.experimental.pallas import tpu as pltpu
from jax.sharding import PartitionSpec as P

CAP = 8
LANES = 128
MIB = 1 << 20
VMEM = pl.BlockSpec(memory_space=pltpu.VMEM)
ANY = pl.BlockSpec(memory_space=pl.ANY)
SMEM = pl.BlockSpec(memory_space=pltpu.SMEM)
BF16 = jnp.bfloat16
F32 = jnp.float32

root_two_pi = math.sqrt(2.0 / math.pi)


def gelu_pair(pre):
    inner = root_two_pi * (pre + 0.044715 * pre * pre * pre)
    tangent = jnp.tanh(inner)
    half = 0.5 * (1.0 + tangent)
    slope = half + 0.5 * pre * (1.0 - tangent * tangent) * root_two_pi * (
        1.0 + 3.0 * 0.044715 * pre * pre
    )
    return pre * half, slope


def dot(left, right, over_left, over_right):
    return lax.dot_general(
        left, right, (((over_left,), (over_right,)), ((), ())), preferred_element_type=F32
    )


def iota(shape, dim):
    return lax.broadcasted_iota(jnp.int32, shape, dim)


def params(mib):
    return pltpu.CompilerParams(vmem_limit_bytes=mib * MIB)


def cost(flops, moved):
    return pl.CostEstimate(flops=flops, bytes_accessed=moved, transcendentals=0)


def slot_hits(expert_ref, slot_ref, kept_ref, slots):
    position = jnp.where(kept_ref[...] == 1, expert_ref[...] * CAP + slot_ref[...], -1)
    return iota((slots, position.shape[1]), 0) == position


CARRIED = (0, 5, 2)


def dispatch_kernel(me_ref, expert_ref, slot_ref, kept_ref, gate_ref, tokens, grad_out, send_ref, x_ref, dy_ref, spread_ref, sems):
    rows, half = send_ref.shape
    loads = [
        pltpu.make_async_copy(tokens, x_ref, sems.at[0]),
        pltpu.make_async_copy(grad_out, dy_ref, sems.at[1]),
    ]
    for load in loads:
        load.start()
    position = jnp.where(kept_ref[...] == 1, expert_ref[...] * CAP + slot_ref[...], -1)
    run = half // len(CARRIED)
    experts = rows // 8
    tile = spread_ref.shape[2]
    tiles = run // tile
    gate_row = gate_ref[...].astype(F32).reshape(1, -1)
    row = iota((len(CARRIED) * experts, position.shape[1]), 0)
    carried = row // experts
    offset = jnp.where(carried == 0, CARRIED[0], jnp.where(carried == 1, CARRIED[1], CARRIED[2]))
    hits = (row - carried * experts) * CAP + ((me_ref[0] + offset) & 7) == position
    for side, (ref, factor) in enumerate(((x_ref, 1.0), (dy_ref, gate_row))):
        pick = jnp.where(hits, factor, 0.0).astype(BF16)
        loads[side].wait()
        for part in range(4):
            r = 4 * side + part
            found = dot(pick, ref[:, part * run : (part + 1) * run], 1, 0)
            for k in range(len(CARRIED)):
                for j in range(tiles):
                    term = found[k * experts : (k + 1) * experts, j * tile : (j + 1) * tile]
                    spread_ref[k * tiles + j, pl.ds(r, experts, stride=8), :] = term
    for j in range(spread_ref.shape[0]):
        send_ref[:, j * tile : (j + 1) * tile] = spread_ref[j].astype(BF16)


def dispatch(me, slots, index_rows, gate, tokens, grad_out):
    count, width = tokens.shape
    tile = min(LANES, width // 4)
    return pl.pallas_call(
        dispatch_kernel,
        out_shape=jax.ShapeDtypeStruct((slots, width // 4 * len(CARRIED)), BF16),
        in_specs=[SMEM] + [VMEM] * 4 + [ANY] * 2,
        out_specs=VMEM,
        scratch_shapes=[
            pltpu.VMEM((count, width), BF16),
            pltpu.VMEM((count, width), BF16),
            pltpu.VMEM((width // 4 * len(CARRIED) // tile, slots, tile), F32),
            pltpu.SemaphoreType.DMA((2,)),
        ],
        compiler_params=params(58),
        cost_estimate=cost(4 * slots * count * width, 5 * slots * width),
    )(me, *index_rows, gate, tokens, grad_out)


def expert_kernel(
    me_ref, data_ref, own, before, after, w_in, w_out, rows, acts, mine,
    own_ref, before_ref, after_ref, x_ref, s_ref, in_ref, out_ref, rows_ref, acts_ref, mine_ref, sems,
):
    slots, width = x_ref.shape
    hidden_width = in_ref.shape[1]
    quarter, part_rows = width // 4, slots // 8
    parts = rows_ref.shape[0]
    loads = [
        pltpu.make_async_copy(own, own_ref, sems.at[0]),
        pltpu.make_async_copy(before, before_ref, sems.at[1]),
        pltpu.make_async_copy(after, after_ref, sems.at[2]),
        pltpu.make_async_copy(w_in, in_ref, sems.at[3]),
        pltpu.make_async_copy(w_out, out_ref, sems.at[4]),
    ]
    for load in loads:
        load.start()
    square = (slots, slots)
    to, at = iota(square, 0), iota(square, 1)
    unpack = jnp.where(at == (to % part_rows) * 8 + to // part_rows, 1.0, 0.0).astype(BF16)
    middle = quarter // 2
    for k, (ref, offset, skip) in enumerate(((own_ref, 0, 0), (before_ref, 7, 0), (after_ref, 1, middle))):
        loads[k].wait()
        plain = dot(unpack, ref[...], 1, 0).astype(BF16)
        for carried, slot_offset in enumerate(CARRIED):
            start = max(carried * quarter, skip)
            end = min((carried + 1) * quarter, skip + ref.shape[1])
            slot = (me_ref[0] + offset + slot_offset) & 7
            place = pl.ds(pl.multiple_of(slot * part_rows, part_rows), part_rows)
            for r in range(8):
                target = (x_ref, s_ref)[r // 4]
                first = (r % 4) * quarter + start - carried * quarter
                target[place, first : first + end - start] = plain[
                    r * part_rows : (r + 1) * part_rows, start - skip : end - skip
                ]
    for k, ref in enumerate((x_ref, x_ref, s_ref, s_ref)):
        for target, mask in ((mine_ref, (0, 2)[k % 2]), (acts_ref, (1, 3)[k % 2])):
            place = pl.ds(pl.multiple_of((data_ref[0] ^ mask) * quarter, quarter), quarter)
            target[:, k * quarter : (k + 1) * quarter] = ref[:, place]
    stores = [
        pltpu.make_async_copy(mine_ref, mine, sems.at[7 + parts]),
        pltpu.make_async_copy(acts_ref, acts, sems.at[8 + parts]),
    ]
    stores[0].start()
    loads[3].wait()
    pre = dot(x_ref[...], in_ref[...], 1, 0)
    loads[4].wait()
    back = dot(s_ref[...], out_ref[...], 1, 1)
    value, slope = gelu_pair(pre)
    hidden = value.astype(BF16)
    acts_ref[:, width + hidden_width :] = hidden
    grad_pre = (back * slope).astype(BF16)
    acts_ref[:, width : width + hidden_width] = grad_pre
    stores[1].start()
    gate = jnp.sum(hidden.astype(F32) * back, axis=1, keepdims=True)
    gate_row = jnp.sum(jnp.where(to == at, gate, 0.0), axis=0, keepdims=True)
    gate_rows = jnp.broadcast_to(gate_row, (16, slots)).astype(BF16)
    block = width // parts
    for part in range(parts):
        term = dot(grad_pre, in_ref[part * block : (part + 1) * block, :], 1, 1)
        rows_ref[part, :slots, :] = term.astype(BF16)
        rows_ref[part, slots:, :] = gate_rows
        stores.append(pltpu.make_async_copy(rows_ref.at[part], rows.at[part], sems.at[7 + part]))
        stores[-1].start()
    for store in stores:
        store.wait()


def expert(me, data, packs, w_in, w_out, parts):
    slots = packs[0].shape[0]
    width, hidden_width = w_in.shape
    outs = (
        (parts, slots + 16, width // parts),
        (slots, width + 2 * hidden_width),
        (slots, width),
    )
    return pl.pallas_call(
        expert_kernel,
        out_shape=tuple(jax.ShapeDtypeStruct(shape, BF16) for shape in outs),
        in_specs=[SMEM, SMEM] + [ANY] * 5,
        out_specs=(ANY, ANY, ANY),
        scratch_shapes=[
            *[pltpu.VMEM(pack.shape, BF16) for pack in packs],
            pltpu.VMEM((slots, width), BF16),
            pltpu.VMEM((slots, width), BF16),
            pltpu.VMEM(w_in.shape, BF16),
            pltpu.VMEM(w_out.shape, BF16),
        ]
        + [pltpu.VMEM(shape, BF16) for shape in outs]
        + [pltpu.SemaphoreType.DMA((9 + parts,))],
        compiler_params=params(52),
        cost_estimate=cost(
            6 * slots * width * hidden_width, 4 * width * (slots + hidden_width) + 8 * slots * width
        ),
    )(me, data, *packs, w_in, w_out)


def sum_kernel(terms_ref, out_ref):
    slots = out_ref.shape[0]
    block = terms_ref.shape[2]
    total = terms_ref[0].astype(F32)
    for part in range(1, terms_ref.shape[0]):
        total = total + terms_ref[part].astype(F32)
    to, at = iota((slots, slots), 0), iota((slots, slots), 1)
    from_row = (to & 7) * (slots // 8) + (to >> 3)
    order = jnp.where(at == from_row, 1.0, 0.0)
    gate = jnp.sum(order * total[slots : slots + 1], axis=1, keepdims=True)
    sums = dot(order.astype(BF16), total[:slots].astype(BF16), 1, 0)
    out_ref[:, :block] = sums.astype(BF16)
    out_ref[:, block:] = jnp.broadcast_to(gate, (slots, LANES)).astype(BF16)


def sum_terms(terms, slots):
    parts, _, block = terms.shape
    return pl.pallas_call(
        sum_kernel,
        out_shape=jax.ShapeDtypeStruct((slots, block + LANES), BF16),
        in_specs=[VMEM],
        out_specs=VMEM,
        compiler_params=params(24),
        cost_estimate=cost(parts * slots * block, 2 * parts * slots * block),
    )(terms)


def finish_kernel(me_ref, expert_ref, slot_ref, kept_ref, gate_ref, home_ref, *refs):
    own_ref, fifth_ref, second_ref, before_ref, after_ref, tokens_ref, gates_ref = refs
    slots, block = own_ref.shape
    hits = slot_hits(expert_ref, slot_ref, kept_ref, slots)
    column = home_ref[:, block : block + 1].astype(F32)
    picked = jnp.sum(jnp.where(hits, column, 0.0), axis=0, keepdims=True)
    gate_row = gate_ref[...].astype(F32).reshape(1, -1)
    gates_ref[...] = (picked / gate_row).astype(BF16).reshape(-1)
    choose = jnp.where(hits, 1.0, 0.0).T.astype(BF16)
    half = slots // 2

    def store(offset, value):
        place = pl.multiple_of(((me_ref[0] + offset) & 7) * block, block)
        tokens_ref[:, pl.ds(place, block)] = value.astype(BF16)

    whole_pieces = (
        (0, own_ref, 0), (5, fifth_ref, 0), (2, second_ref, 0),
        (7, before_ref, 0), (4, before_ref, slots), (6, after_ref, half), (3, after_ref, slots + half),
    )
    for offset, ref, start in whole_pieces:
        store(offset, dot(choose, ref[start : start + slots, :], 1, 0))
    low = dot(choose[:, :half], before_ref[2 * slots :, :], 1, 0)
    store(1, low + dot(choose[:, half:], after_ref[:half, :], 1, 0))


def finish(me, index_rows, gate, home, pieces, width):
    count = gate.shape[0]
    return pl.pallas_call(
        finish_kernel,
        out_shape=(
            jax.ShapeDtypeStruct((count, width), BF16),
            jax.ShapeDtypeStruct((count,), BF16),
        ),
        in_specs=[SMEM] + [VMEM] * (5 + len(pieces)),
        out_specs=(VMEM, VMEM),
        compiler_params=params(24),
        cost_estimate=cost(2 * count * count * width, 4 * count * width),
    )(me, *index_rows, gate, home, *pieces)


def term(left, mine_ref, acts_ref, other_ref, turn, first, activations):
    quarter = mine_ref.shape[1] // 4
    cols = slice((turn + first) * quarter, (turn + first + 1) * quarter)
    total = None
    for rows_ref, from_ref in ((mine_ref, acts_ref), (other_ref, other_ref)):
        pair = rows_ref[:, cols], from_ref[:, activations]
        product = dot(*(pair if left else pair[::-1]), 0, 0)
        total = product if total is None else total + product
    return total


def pass_kernel(mine_ref, acts_ref, other_ref, out_ref):
    quarter, width = mine_ref.shape[1] // 4, out_ref.shape[1]
    grads = slice(4 * quarter, 4 * quarter + width)
    hiddens = slice(4 * quarter + width, 4 * quarter + 2 * width)
    out_ref[:quarter] = term(True, mine_ref, acts_ref, other_ref, 1, 0, grads).astype(BF16)
    out_ref[quarter:] = term(True, mine_ref, acts_ref, other_ref, 1, 2, hiddens).astype(BF16)


def keep_kernel(mine_ref, acts_ref, other_ref, added_ref, in_ref, out_ref):
    quarter, width = in_ref.shape
    grads = slice(4 * quarter, 4 * quarter + width)
    hiddens = slice(4 * quarter + width, 4 * quarter + 2 * width)
    first = term(True, mine_ref, acts_ref, other_ref, 0, 0, grads)
    in_ref[...] = (first + added_ref[:quarter].astype(F32)).astype(BF16)
    second = term(False, mine_ref, acts_ref, other_ref, 0, 2, hiddens)
    out_ref[...] = (second + added_ref[quarter:].astype(F32).T).astype(BF16)


def weight_terms(mine, acts, other, added=None):
    slots = mine.shape[0]
    quarter = mine.shape[1] // 4
    width = (acts.shape[1] - 4 * quarter) // 2
    shapes = ((2 * quarter, width),) if added is None else ((quarter, width), (width, quarter))
    args = (mine, acts, other) if added is None else (mine, acts, other, added)
    return pl.pallas_call(
        pass_kernel if added is None else keep_kernel,
        in_specs=[VMEM] * len(args),
        out_specs=(VMEM,) * len(shapes),
        out_shape=tuple(jax.ShapeDtypeStruct(shape, BF16) for shape in shapes),
        compiler_params=params(24 if added is None else 24),
        cost_estimate=cost(8 * slots * quarter * width, 8 * slots * (quarter + width) + 4 * quarter * width),
    )(*args)


def shift(value, step):
    return lax.ppermute(value, "mp", [(i, (i + step) % 8) for i in range(8)])


def swap(value, bit):
    return lax.ppermute(value, "dp", [(i, i ^ bit) for i in range(4)])


def gather_pieces(piece):
    held = piece, shift(piece, 3), shift(piece, -2)
    half = piece.shape[0] // 2
    before = jnp.concatenate([held[0], held[1], held[2][:half]])
    after = jnp.concatenate([held[0][half:], held[1], held[2]])
    return held + (shift(before, 1), shift(after, -1))


def scatter(value, axis):
    return lax.all_to_all(value, axis, split_axis=0, concat_axis=0, tiled=True)


def local(grad_out, tokens, gate, expert_index, slot, kept, w_in, w_out):
    experts = lax.axis_size("expert")
    parts = lax.axis_size("mp")
    count, width = tokens.shape
    slots = experts * CAP
    index_rows = [value.reshape(1, count) for value in (expert_index, slot, kept)]
    me = lax.axis_index("mp").astype(jnp.int32).reshape(1)
    data = lax.axis_index("dp").astype(jnp.int32).reshape(1)

    send = dispatch(me, slots, index_rows, gate, tokens, grad_out)
    came = scatter(send.reshape(experts, CAP, send.shape[1]), "expert").reshape(send.shape)
    middle = width // 8
    packs = (came, shift(came[:, : came.shape[1] - middle], 1), shift(came[:, middle:], -1))
    rows, acts, mine = expert(me, data, packs, w_in[0], w_out[0], parts)
    terms = scatter(rows, "mp")

    other = swap(acts, 1)
    added = swap(weight_terms(mine, acts, other)[0], 2)

    total = sum_terms(terms, slots)
    home = scatter(total.reshape(experts, CAP, total.shape[1]), "expert").reshape(total.shape)
    home, added = lax.optimization_barrier((home, added))
    grad_w_in, grad_w_out = weight_terms(mine, acts, other, added)
    pieces = gather_pieces(home[:, : width // parts])
    grad_tokens, grad_gate = finish(me, index_rows, gate, home, pieces, width)
    return (grad_tokens, grad_gate, grad_w_in[None], grad_w_out[None])


def solution(mesh):
    placed = (
        P(("expert", "dp"), None),
        P(("expert", "dp"), None),
        P(("expert", "dp")),
        P(("expert", "dp")),
        P(("expert", "dp")),
        P(("expert", "dp")),
        P("expert", None, "mp"),
        P("expert", "mp", None),
    )
    return jax.shard_map(
        local,
        mesh=mesh,
        in_specs=placed,
        out_specs=(
            P(("expert", "dp"), None),
            P(("expert", "dp")),
            P("expert", "dp", "mp"),
            P("expert", "mp", "dp"),
        ),
        check_vma=False,
    )
```
